1024 devices in a mesh: gx: 16 (over z_lo, core), gy: 8 (over y), gz: 8 (over x, z_hi).
Axes of the slice: x: 4, y: 8, z: 16 (z_hi: 2, z_lo: 8; z = z_hi * 8 + z_lo), core: 2. Of those that a mesh axis runs over, the one named last changes fastest.
Arguments:
- positions: float32 [16, 8, 8, 3, 128], P('gx', 'gy', 'gz'), may hold values from 0 to 10
- species: int32 [16, 8, 8, 128], P('gx', 'gy', 'gz'), may hold values from 0 to 7
- send_list: int32 [16, 8, 8, 2, 64], P('gx', 'gy', 'gz'), may hold values from 0 to 127, as said below
- send_count: int32 [16, 8, 8, 2], P('gx', 'gy', 'gz'), may hold values from 1 to 64, as said below
- pair_list: int32 [16, 8, 8, 8, 2], P('gx', 'gy', 'gz'), may hold values from 0 to 107, as said below
- pair_count: int32 [16, 8, 8], P('gx', 'gy', 'gz'), may hold values from 1 to 8, as said below
- w_radial: float32 [8, 64], replicated, may hold values from -2 to 2
- species_emb: float32 [8, 64], replicated, may hold values from -4 to 4
- w_first: bfloat16 [256, 512], replicated, may hold values from -0.375 to 0.375
- w_second: bfloat16 [512, 512], replicated, may hold values from -0.25 to 0.25
- w_out: float32 [512], replicated, may hold values from -0.25 to 0.25
Outputs:
- forces: float32 [16, 8, 8, 3, 256], P('gx', 'gy', 'gz')
- atom_energy: float32 [16, 8, 8, 256], P('gx', 'gy', 'gz')
The draws below stay inside these ranges and needn't reach their ends.
Inputs may be any that keep to these rules, and one draw needn't show every extreme that they name: `send_list`: within one cell the first send_count entries of both lists together name distinct atoms. `send_count`: some cell fills a list. `pair_list`: column 0 is below 4; only the first pair_count rows of a cell are used. `pair_count`: some cell uses all slots.
All inputs are finite; a program needn't handle non-finite values.
Results may differ from the reference program's by a relative error of at most 0.018.
Values sent between devices are 32-bit elements; how exact they have to be, the bound alone decides.
A program may use at most 32 MiB of HBM per device.

```python
import jax
import jax.numpy as jnp
from jax import lax

ATOM_DEV = 128
MIG = 64
TILE = 64
PAIRS = 8
CHANNELS = 64
HIDDEN_SIZE = 512
NB = 8
SPECIES = 8
TILES = 4
N_GX = 16
N_GY = 8
N_GZ = 8


def draw_send_list(key, part):
    key = jax.random.fold_in(key, 11)
    scores = jax.random.randint(key, (N_GX, N_GY, N_GZ, ATOM_DEV), 0, 65536) * ATOM_DEV + jnp.arange(ATOM_DEV)
    ordering = jnp.argsort(scores, axis=-1, stable=True).astype(jnp.int32)
    return ordering[..., :2 * MIG].reshape(N_GX, N_GY, N_GZ, 2, MIG)


def draw_send_count(key, part):
    key = jax.random.fold_in(key, 23)
    counts = jax.random.randint(key, (N_GX, N_GY, N_GZ, 2), 1, MIG + 1)
    return counts.at[0, 0, 0, 0].set(MIG).astype(jnp.int32)


def draw_pair_list(key, part):
    key = jax.random.fold_in(key, 37)
    key_centre, key_which, key_near, key_far, key_tile = jax.random.split(key, 5)
    shape = (N_GX, N_GY, N_GZ, PAIRS)
    centre_col = jax.random.randint(key_centre, shape, 0, TILES)
    nearby = jnp.array([13, 4, 10, 12, 14, 16, 22], jnp.int32)
    which = jax.random.randint(key_which, shape, 0, 2)
    near_block = nearby[jax.random.randint(key_near, shape, 0, 7)]
    far_block = jax.random.randint(key_far, shape, 0, 27)
    block = jnp.where(which == 0, near_block, far_block)
    other_col = block * TILES + jax.random.randint(key_tile, shape, 0, TILES)
    other_col = other_col.at[0, 0, 0, 0].set(27 * TILES - 1)
    return jnp.stack([centre_col, other_col], -1).astype(jnp.int32)


def draw_pair_count(key, part):
    key = jax.random.fold_in(key, 41)
    counts = jax.random.randint(key, (N_GX, N_GY, N_GZ), 1, PAIRS + 1)
    return counts.at[0, 0, 0].set(PAIRS).astype(jnp.int32)


def with_ends(drawn, rng, smallest, largest):
    longest = drawn.shape.index(max(drawn.shape))
    spots = []
    for shift in (0, 1):
        where = [jax.random.randint(jax.random.fold_in(rng, axis), (), 0, length) for axis, length in enumerate(drawn.shape)]
        where[longest] = (where[longest] + shift) % drawn.shape[longest]
        spots.append(tuple(where))
    return drawn.at[spots[0]].set(smallest).at[spots[1]].set(largest)


def block_scale(rng, dims, cuts, low, top_value):
    def one(axis_at, blocks):
        heights = jax.random.uniform(jax.random.fold_in(jax.random.fold_in(rng, 6), axis_at), (blocks,), jnp.float32, low / len(cuts), top_value / len(cuts))
        return jnp.repeat(jnp.exp(heights), dims[axis_at] // blocks).reshape((-1,) + (1,) * (len(dims) - axis_at - 1))

    level = one(*cuts[0])
    for cut in cuts[1:]:
        level = level * one(*cut)
    return level


def scatter_about(rng, shape, spread, most, kind=jnp.bfloat16):
    values = spread * jax.random.normal(rng, shape, jnp.float32)
    return jnp.clip(values, min=-most, max=most).astype(kind)


def setup_inputs(seed: int = 0) -> dict:
    seeds = jax.random.split(jax.random.key(seed), 12)
    return {
        "positions": jnp.clip(10.0 * jax.random.uniform(seeds[0], (N_GX, N_GY, N_GZ, 3, ATOM_DEV), jnp.float32) ** block_scale(seeds[0], (N_GX, N_GY, N_GZ, 3, ATOM_DEV), ((0, 16), (1, 8), (2, 8)), -0.2, 0.2), 0.0, 10.0),
        "species": with_ends(jax.random.randint(seeds[1], (N_GX, N_GY, N_GZ, ATOM_DEV), 0, SPECIES), jax.random.fold_in(seeds[1], 1), 0, SPECIES - 1).astype(jnp.int32),
        "send_list": draw_send_list(jax.random.fold_in(seeds[11], 71), 0),
        "send_count": draw_send_count(jax.random.fold_in(seeds[11], 71), 0),
        "pair_list": draw_pair_list(jax.random.fold_in(seeds[11], 71), 0),
        "pair_count": draw_pair_count(jax.random.fold_in(seeds[11], 71), 0),
        "w_radial": scatter_about(seeds[6], (NB, CHANNELS), NB ** -0.5, 2.0, jnp.float32),
        "species_emb": scatter_about(seeds[7], (SPECIES, CHANNELS), 1.0, 4.0, jnp.float32),
        "w_first": scatter_about(seeds[8], (4 * CHANNELS, HIDDEN_SIZE), (4 * CHANNELS) ** -0.5, 0.375),
        "w_second": scatter_about(seeds[9], (HIDDEN_SIZE, HIDDEN_SIZE), HIDDEN_SIZE ** -0.5, 0.25),
        "w_out": scatter_about(seeds[10], (HIDDEN_SIZE,), HIDDEN_SIZE ** -0.5, 0.25, jnp.float32),
    }


cell = 10.0
cutoff = 5.0
cutoff_sq = 25.0
soften = 0.25
sharpness = 1.0
env_scale = 0.5

def offsets_grid():
    stepping = (jnp.arange(3, dtype=jnp.float32) - 1.0) * cell
    zeroes = jnp.zeros((3, 3, 3), jnp.float32)
    return jnp.stack([zeroes + stepping[:, None, None], zeroes + stepping[None, :, None], zeroes + stepping[None, None, :]], 3)[..., None]

def depart(packed, lists, counts):
    capacity = lists.shape[-1]
    live_slot = jnp.arange(capacity)[None, :] < counts[:, None]
    buffers = packed[:, lists]
    kind_row = jnp.where(live_slot[None], buffers[3:4], -1.0)
    buffers = jnp.concatenate([buffers[:3], kind_row], 0)
    leaving = (lists[:, :, None] == jnp.arange(packed.shape[1])[None, None, :]) & live_slot[:, :, None]
    leaving = jnp.any(leaving, axis=(0, 1))
    staying = jnp.concatenate([packed[:3], jnp.where(leaving, -1.0, packed[3])[None]], 0)
    return (buffers[:, 0], buffers[:, 1], staying)

def tile_environment(centre_tile, other_tile, same_tile, w_radial, species_emb):
    delta = other_tile[:3, None, :] - centre_tile[:3, :, None]
    squared = lax.optimization_barrier(jnp.sum(delta * delta, axis=0))
    distance = jnp.sqrt(squared + soften)
    unit_x = delta[0] / distance
    unit_y = delta[1] / distance
    unit_z = delta[2] / distance
    both_live = (centre_tile[3] >= 0).astype(jnp.float32)[:, None] * (other_tile[3] >= 0).astype(jnp.float32)[None, :]
    diagonal = jnp.eye(TILE, dtype=jnp.float32) * same_tile.astype(jnp.float32)
    inside = jnp.maximum(1.0 - squared / cutoff_sq, 0.0)
    envelope = inside * inside * both_live * (1.0 - diagonal)
    centres = (jnp.arange(NB, dtype=jnp.float32) + 1.0) * (cutoff / NB)
    radial_basis = jnp.exp(-sharpness * (distance[:, :, None] - centres) ** 2) * envelope[:, :, None]
    harmonics = jnp.stack([jnp.ones_like(unit_x), unit_x, unit_y, unit_z, unit_x * unit_y, unit_y * unit_z, 1.5 * unit_z * unit_z - 0.5, unit_x * unit_z, 0.5 * (unit_x * unit_x - unit_y * unit_y)], -1)
    mixed = (radial_basis[:, :, :, None] * harmonics[:, :, None, :]).reshape(TILE, TILE, NB * 9)
    species_hot = (other_tile[3][:, None] == jnp.arange(SPECIES, dtype=jnp.float32)[None, :]).astype(jnp.float32)
    neighbour_embed = jnp.dot(species_hot, species_emb, precision=lax.Precision.HIGHEST)
    gathered = jnp.einsum('ijx,jc->ixc', mixed, neighbour_embed, precision=lax.Precision.HIGHEST)
    gathered = gathered.reshape(TILE, NB, 9, -1)
    return jnp.einsum('inmc,nc->icm', gathered, w_radial, precision=lax.Precision.HIGHEST)

def local_energy(extended, pair_rows, pair_total, w_radial, species_emb, w_first, w_second, w_out):
    width = extended.shape[-1]
    tile_count = width // TILE
    channels = species_emb.shape[1]
    pieces = extended.reshape(27, 4, tile_count, TILE).transpose(0, 2, 1, 3).reshape(27 * tile_count, 4, TILE)
    centre_base = 13 * tile_count
    visit_tile = jax.checkpoint(tile_environment)

    def visit(running, entry):
        pair_row, position = entry
        centre_index = centre_base + pair_row[0]
        contribution = visit_tile(pieces[centre_index], pieces[pair_row[1]], pair_row[1] == centre_index, w_radial, species_emb)
        active = (position < pair_total).astype(jnp.float32)
        select = (jnp.arange(tile_count) == pair_row[0]).astype(jnp.float32) * active
        return (running + select[:, None, None, None] * contribution[None], None)
    start_env = jnp.zeros((tile_count, TILE, channels, 9), jnp.float32)
    environment, _ = lax.scan(visit, start_env, (pair_rows, jnp.arange(pair_rows.shape[0])))
    environment = environment.reshape(width, channels, 9) * env_scale
    invariants = jnp.concatenate([environment[:, :, 0] ** 2, lax.optimization_barrier(jnp.sum(environment[:, :, 1:4] ** 2, -1)), lax.optimization_barrier(jnp.sum(environment[:, :, 4:] ** 2, -1))], -1)
    centre_kinds = extended[13, 3]
    centre_live = (centre_kinds >= 0).astype(jnp.float32)
    centre_hot = (centre_kinds[:, None] == jnp.arange(SPECIES, dtype=jnp.float32)[None, :]).astype(jnp.float32)
    centre_embed = jnp.dot(centre_hot, species_emb, precision=lax.Precision.HIGHEST)
    features = jnp.concatenate([invariants, centre_embed], -1).astype(jnp.bfloat16)
    first_layer = jax.nn.silu(jnp.dot(features, w_first, preferred_element_type=jnp.float32)).astype(jnp.bfloat16)
    second_layer = jax.nn.silu(jnp.dot(first_layer, w_second, preferred_element_type=jnp.float32)).astype(jnp.bfloat16)
    return jnp.dot(second_layer.astype(jnp.float32), w_out, precision=lax.Precision.HIGHEST) * centre_live

def reference(positions, species, send_list, send_count, pair_list, pair_count, w_radial, species_emb, w_first, w_second, w_out):
    grid_x, grid_y, grid_z = positions.shape[:3]
    cells = grid_x * grid_y * grid_z
    packed = jnp.concatenate([positions, species.astype(jnp.float32)[:, :, :, None, :]], 3)
    to_lower, to_upper, staying = jax.vmap(depart)(packed.reshape(cells, 4, -1), send_list.reshape(cells, 2, -1), send_count.reshape(cells, 2))
    to_lower = to_lower.reshape(grid_x, grid_y, grid_z, 4, -1)
    to_upper = to_upper.reshape(grid_x, grid_y, grid_z, 4, -1)
    staying = staying.reshape(grid_x, grid_y, grid_z, 4, -1)
    from_lower = jnp.roll(to_upper, 1, axis=0)
    from_lower = from_lower.at[:, :, :, 0].add(-cell)
    from_upper = jnp.roll(to_lower, -1, axis=0)
    from_upper = from_upper.at[:, :, :, 0].add(cell)
    fresh = jnp.concatenate([from_lower, staying, from_upper], -1)
    coords = fresh[:, :, :, :3]
    kinds = fresh[:, :, :, 3:4]

    def energy_of(coordinates):
        whole = jnp.concatenate([coordinates, kinds], 3)
        blocks = []
        for shift_a in range(3):
            for shift_b in range(3):
                for shift_c in range(3):
                    blocks.append(jnp.roll(whole, (1 - shift_a, 1 - shift_b, 1 - shift_c), axis=(0, 1, 2)))
        extended = jnp.stack(blocks, 3)
        extended = extended.at[:, :, :, :, :3].add(offsets_grid().reshape(27, 3, 1))
        flat_ext = extended.reshape(cells, 27, 4, -1)

        def per_cell(entry):
            return local_energy(entry[0], entry[1], entry[2], w_radial, species_emb, w_first, w_second, w_out)
        energies = lax.map(jax.checkpoint(per_cell), (flat_ext, pair_list.reshape(cells, pair_list.shape[3], 2), pair_count.reshape(cells)))
        return energies.reshape(grid_x, grid_y, grid_z, -1)
    energies, pullback = jax.vjp(energy_of, coords)
    gradient, = pullback(jnp.ones_like(energies))
    return (-gradient, energies)
```

```python
import functools

import jax
import jax.numpy as jnp
from jax import lax
from jax.experimental import pallas as pl
from jax.experimental.pallas import tpu as pltpu
from jax.sharding import PartitionSpec as P

TILE = 64
NB = 8
PAIRS = 8
SPECIES = 8
CHANNELS = 64
HARM = 9
EDGE = PAIRS * TILE
HALF = EDGE // 2

cell = 10.0
cutoff = 5.0
cutoff_sq = 25.0
soften = 0.25
sharpness = 1.0
env_scale = 0.5

MESH = pl.DeviceIdType.MESH
F32 = jnp.float32
BF16 = jnp.bfloat16

PLANE_FAR = [(a, b) for a in (-2, -1, 0, 1, 2) for b in (-1, 0, 1)]

E_UX, E_UY, E_UZ, E_D, E_INV, E_F, E_SLOPE = range(NB, NB + 7)


def slot_far(a, b):
    return (a + 2) * 3 + (b + 1)


def block_of(a, b, c):
    return (a + 1) * 9 + (b + 1) * 3 + (c + 1)


def iota(shape, dim):
    return lax.broadcasted_iota(jnp.int32, shape, dim)


def three_parts(value):
    high = value.astype(BF16)
    rest = value - high.astype(F32)
    middle = rest.astype(BF16)
    low = (rest - middle.astype(F32)).astype(BF16)
    return high, middle, low


def pick(hot, value, dims):
    total = None
    for part in three_parts(value):
        term = lax.dot_general(hot, part, (dims, ((), ())), preferred_element_type=F32)
        total = term if total is None else total + term
    return total


def contract(left, right, dims):
    return lax.dot_general(left, right, (dims, ((), ())), preferred_element_type=F32)


def kernel(
    sizes,
    pos_hbm,
    kind_hbm,
    list_hbm,
    sent_hbm,
    pair_hbm,
    total_hbm,
    radial_hbm,
    emb_hbm,
    out_hbm,
    first_hbm,
    second_hbm,
    force_ref,
    pos_ref,
    kind_ref,
    list_ref,
    sent_ref,
    pair_ref,
    total_ref,
    radial_ref,
    emb_ref,
    out_ref,
    packed,
    raw,
    rim_out,
    rim_in,
    plane,
    asked_own,
    asked,
    tiles_out,
    tiles_in,
    back_out,
    back_in,
    w_first,
    w_second,
    mix,
    terms,
    back_terms,
    edges,
    centre_at,
    env,
    env_grad,
    features,
    hidden,
    slope,
    pull,
    push,
    send_sem,
    recv_sem,
    load_sem,
):
    here = {axis: lax.axis_index(axis) for axis in ("gx", "gy", "gz")}

    def at(a, b, c):
        return {
            axis: lax.rem(here[axis] + (step + sizes[axis]), sizes[axis])
            for axis, step in (("gx", a), ("gy", b), ("gz", c))
        }

    far = [where for where in PLANE_FAR if where != (0, 0)]
    around = [(a, b, c) for c in (-1, 1, 0) for a in (-1, 0, 1) for b in (-1, 0, 1)]
    around.remove((0, 0, 0))

    barrier = pltpu.get_barrier_semaphore()
    for c in (-1, 1):
        pl.semaphore_signal(barrier, inc=1, device_id=at(0, 0, c), device_id_type=MESH)
    for a, b in far:
        pl.semaphore_signal(barrier, inc=1, device_id=at(a, b, 0), device_id_type=MESH)

    loads = []
    for src, dst in (
        (list_hbm, list_ref),
        (pos_hbm, pos_ref),
        (kind_hbm, kind_ref),
        (sent_hbm, sent_ref),
        (pair_hbm, pair_ref),
        (total_hbm, total_ref),
        (emb_hbm, emb_ref),
        (radial_hbm, radial_ref),
        (first_hbm, w_first),
        (second_hbm, w_second),
        (out_hbm, out_ref),
    ):
        copy = pltpu.make_async_copy(src, dst, load_sem.at[len(loads)])
        copy.start()
        loads.append(copy)
    load_emb, load_radial, load_first, load_second, load_out = loads[6:]
    plane[...] = jnp.zeros(plane.shape, F32)
    for copy in loads[:6]:
        copy.wait()

    counter = [0]

    def remote(src, dst, where, landing):
        index = counter[0]
        counter[0] += 1
        return pltpu.make_async_remote_copy(
            src_ref=src,
            dst_ref=dst,
            send_sem=send_sem.at[index],
            recv_sem=recv_sem.at[landing],
            device_id=at(*where),
            device_id_type=MESH,
        )

    lane = iota((1, 2 * TILE), 1)
    left_half = lane < TILE
    sub = iota((8, 2 * TILE), 0)

    def swap(value):
        return pltpu.roll(value, TILE, axis=value.ndim - 1)

    packed[0:1, :] = pos_ref[0]
    packed[1:2, :] = pos_ref[1]
    packed[2:3, :] = pos_ref[2]
    packed[3:4, :] = kind_ref[...].astype(F32)
    packed[4:8, :] = jnp.zeros((4, 2 * TILE), F32)
    atoms = packed[...]
    lists = list_ref[...]
    named = jnp.concatenate([lists[1:2], lists[0:1]], axis=1)
    live_lanes = jnp.where(left_half, sent_ref[0, 1], sent_ref[0, 0] + TILE)
    live = (lane < live_lanes).astype(F32)
    hot = (iota((2 * TILE, 2 * TILE), 0) == named).astype(F32).astype(BF16)
    leaving = contract(
        jnp.broadcast_to(live, (16, 2 * TILE)).astype(BF16), hot, ((1,), (1,))
    )[0:8]
    stacked = jnp.concatenate([part.astype(F32) for part in three_parts(atoms)], axis=0)
    stacked = jnp.concatenate([stacked, jnp.zeros((8, 2 * TILE), F32)], axis=0).astype(BF16)
    moved = contract(stacked, hot, ((1,), (0,)))
    moved = moved[0:8] + moved[8:16] + moved[16:24]
    moved = jnp.where((sub == 3) & (live < 0.5), -1.0, moved)
    staying = jnp.where((sub == 3) & (leaving > 0.5), -1.0, atoms)
    own = slot_far(0, 0)
    moved_swap = swap(moved)
    staying_swap = swap(staying)

    def put_row(row, one, other):
        raw[own, row : row + 1, 0:128] = jnp.where(left_half, one[0:1], other[1:2])
        raw[own, row : row + 1, 128:256] = jnp.where(left_half, one[2:3], other[3:4])

    put_row(0, moved, moved_swap)
    put_row(1, staying, staying_swap)
    put_row(2, staying_swap, staying)
    put_row(3, moved_swap, moved)
    rim_out[0] = raw[own, 0:1, :]
    rim_out[1] = raw[own, 3:4, :]

    pair_total = total_ref[0, 0, 0]
    want = jnp.full((8, 128), -1, jnp.int32)
    want_centre = jnp.full((8, 128), -1, jnp.int32)
    level = jnp.zeros((8, 128), jnp.int32)
    centres = []
    for p in range(PAIRS):
        active = p < pair_total
        centre = jnp.where(active, pair_ref[0, p], -1)
        other = jnp.where(active, pair_ref[1, p], -1)
        centres.append(centre)
        want = jnp.where(sub == p, other, want)
        want_centre = jnp.where(sub == p, jnp.where(active, centre + 13 * 4, -1), want_centre)
        level = jnp.where(sub == p, lax.rem(lax.div(other + 12, 4), 3) - 1, level)
    want = want.astype(F32)
    want_centre = want_centre.astype(F32)
    asked_own[...] = want

    pl.semaphore_wait(barrier, len(far) + 2)

    ask = [
        remote(asked_own, asked.at[1], (0, 0, -1), 0),
        remote(asked_own, asked.at[0], (0, 0, 1), 1),
    ]
    for copy in ask:
        copy.start()
    ghosts = []
    rims = []
    for a, b in sorted(far, key=lambda where: -abs(where[0])):
        landing = slot_far(-a, -b)
        if abs(a) == 2:
            side = 0 if a > 0 else 1
            place = side * 3 + (1 - b)
            copy = remote(rim_out.at[side], rim_in.at[place], (a, b, 0), 2 + landing)
            rims.append((copy, place, side, -a, -b))
        else:
            copy = remote(raw.at[own], raw.at[landing], (a, b, 0), 2 + landing)
            ghosts.append((copy, -a, -b))
        copy.start()

    load_emb.wait()
    load_radial.wait()
    wide = iota((1, 4 * TILE), 1)
    tile_of_lane = lax.shift_right_logical(wide, 6)
    emb = emb_ref[...]
    emb_twice = jnp.concatenate([emb, emb], axis=1)
    radial_twice = jnp.concatenate([radial_ref[...], radial_ref[...]], axis=1)
    emb_wide = jnp.concatenate([emb_twice, emb_twice], axis=1) * env_scale
    radial_wide = jnp.concatenate([radial_twice, radial_twice], axis=1)
    chosen = [(tile_of_lane == centres[p]).astype(F32) for p in range(PAIRS)]
    table = []
    for n in range(NB):
        base = emb_wide * radial_wide[n : n + 1]
        table.append(
            jnp.concatenate([base * chosen[p] for p in range(PAIRS)], axis=0).astype(BF16)
        )

    edge_lane = iota((8, EDGE), 1)
    edge_pair = lax.shift_right_logical(edge_lane, 6)
    pair_mask = edge_pair == iota((8, EDGE), 0)
    pair_hot = pair_mask.astype(F32)

    wide_xy = lax.shift_right_logical(wide, 6)

    def shifted(a, b):
        return jnp.where(wide_xy == 0, a * cell, 0.0) + jnp.where(wide_xy == 1, b * cell, 0.0)

    plane[4 * own : 4 * own + 4, :] = raw[own]
    for copy, a, b in ghosts:
        copy.wait_recv()
        k = slot_far(a, b)
        plane[4 * k : 4 * k + 4, :] = raw[k] + shifted(float(a), float(b))
    for copy, place, side, a, b in rims:
        copy.wait_recv()
        k = 4 * slot_far(a, b) + 3 * side
        plane[k : k + 1, :] = rim_in[place] + shifted(float(a), float(b))
    for copy in ask:
        copy.wait_recv()

    row = iota((1, 64), 1)
    part = jnp.bitwise_and(row, 3)
    block = lax.shift_right_logical(row, 2)
    far_x = lax.shift_right_logical(block * 11, 5)
    far_y = block - far_x * 3
    near_x = far_x - 1 + (part == 0).astype(jnp.int32) - (part == 3).astype(jnp.int32)
    raw_ok = (near_x >= 0) & (near_x <= 2) & (block < 15)
    raw_base = jnp.where(raw_ok, (9 * near_x + 3 * far_y) * 4 + part, -100)

    def asked_rows(base, parts):
        return jnp.concatenate(
            [
                (values[:, :64] == (base + 4 * (c + 1)).astype(F32)).astype(F32)
                for values, c in parts
            ],
            axis=0,
        ).astype(BF16)

    lower = asked[0]
    upper = asked[1]
    which = asked_rows(raw_base, [(want, 0), (lower, 1), (upper, -1), (want_centre, 0)])
    picked = pick(which, plane[...], ((1,), (0,)))
    tiles_out[0] = picked[8:16]
    tiles_out[1] = picked[16:24]
    fetch = [
        remote(tiles_out.at[0], tiles_in.at[1], (0, 0, -1), 17),
        remote(tiles_out.at[1], tiles_in.at[0], (0, 0, 1), 18),
    ]
    for copy in fetch:
        copy.start()

    pair_hot16 = pair_hot.astype(BF16)
    spread = None
    for piece in three_parts(picked[24:32]):
        term = contract(piece, pair_hot16, ((0,), (0,)))
        spread = term if spread is None else spread + term
    centre_at[...] = spread

    tile_rows = [
        plane[4 * slot_far(-1, 0) : 4 * slot_far(-1, 0) + 1, 128:256],
        plane[4 * own + 1 : 4 * own + 2, 128:256],
        plane[4 * own + 2 : 4 * own + 3, 128:256],
        plane[4 * slot_far(1, 0) + 3 : 4 * slot_far(1, 0) + 4, 128:256],
    ]
    kinds = jnp.concatenate(
        [
            jnp.where(left_half, swap(tile_rows[0]), tile_rows[1]),
            jnp.where(left_half, swap(tile_rows[2]), tile_rows[3]),
        ],
        axis=1,
    )
    kind_hot = (kinds == iota((SPECIES, 256), 0).astype(F32)).astype(F32).astype(BF16)
    centre_emb = contract(kind_hot, emb_twice.astype(BF16), ((0,), (0,)))

    def pair_row(values):
        tiled = jnp.concatenate([values] * 4, axis=1)
        return jnp.sum(jnp.where(pair_mask, tiled, 0.0), axis=0, keepdims=True)

    same = pair_row((want == want_centre).astype(F32))
    centre_row = jnp.zeros((1, EDGE), jnp.int32) - 1
    for p in range(PAIRS):
        centre_row = jnp.where(edge_pair[0:1] == p, centres[p], centre_row)
    centre_hot = (centre_row == iota((16, EDGE), 0)).astype(F32).astype(BF16)
    lane_j = jnp.bitwise_and(edge_lane[0:1], TILE - 1)

    for copy in fetch:
        copy.wait_recv()
    lift = jnp.where(left_half, level.astype(F32) * cell, 0.0)
    others = picked[0:8] + tiles_in[0] + tiles_in[1]
    xy = others[:, :128]
    zs = others[:, 128:256] + lift
    xy_swap = swap(xy)
    zs_swap = swap(zs)
    other_x = pair_row(jnp.where(left_half, xy, xy_swap))
    other_y = pair_row(jnp.where(left_half, xy_swap, xy))
    other_z = pair_row(jnp.where(left_half, zs, zs_swap))
    other_kind = pair_row(jnp.where(left_half, zs_swap, zs))
    other_live = (other_kind >= 0).astype(F32)

    kind_rows = iota((SPECIES, EDGE), 0).astype(F32)
    of_kind = (other_kind == kind_rows).astype(F32)
    other_hot = jnp.concatenate(
        [of_kind * (edge_pair == p).astype(F32) for p in range(PAIRS)], axis=0
    ).astype(BF16)
    for n in range(NB):
        mix[n * EDGE : (n + 1) * EDGE, :] = contract(
            other_hot, table[n], ((0,), (0,))
        ).astype(BF16)

    spots = [cutoff * (n + 1) / NB for n in range(NB)]

    def forward(step, carry):
        start = pl.multiple_of(step * 16, 16)
        rows = pl.ds(start, 16)
        row_i = iota((16, HALF), 0) + start
        for g in range(2):
            cols = slice(g * HALF, (g + 1) * HALF)
            dx = other_x[:, cols] - centre_at[pl.ds(start, 16), cols]
            dy = other_y[:, cols] - centre_at[pl.ds(start + TILE, 16), cols]
            dz = other_z[:, cols] - centre_at[pl.ds(start + 2 * TILE, 16), cols]
            kind_i = centre_at[pl.ds(start + 3 * TILE, 16), cols]
            squared = dx * dx + dy * dy + dz * dz
            inverse = lax.rsqrt(squared + soften)
            distance = (squared + soften) * inverse
            keep = jnp.where(kind_i >= 0, other_live[:, cols], 0.0)
            keep = jnp.where((row_i == lane_j[:, cols]) & (same[:, cols] > 0.5), 0.0, keep)
            inside = jnp.maximum(1.0 - squared * (1.0 / cutoff_sq), 0.0)
            slope_f = inside * keep
            envelope = inside * slope_f
            ux = dx * inverse
            uy = dy * inverse
            uz = dz * inverse
            edges[E_UX, rows, cols] = ux
            edges[E_UY, rows, cols] = uy
            edges[E_UZ, rows, cols] = uz
            edges[E_D, rows, cols] = distance
            edges[E_INV, rows, cols] = inverse
            edges[E_F, rows, cols] = envelope
            edges[E_SLOPE, rows, cols] = slope_f
            harmonics = [
                None,
                ux,
                uy,
                uz,
                ux * uy,
                uy * uz,
                1.5 * uz * uz - 0.5,
                ux * uz,
                0.5 * (ux * ux - uy * uy),
            ]
            for n in range(NB):
                away = distance - spots[n]
                bump = jnp.exp(-sharpness * away * away)
                edges[n, rows, cols] = bump
                radial = bump * envelope
                depth = slice(n * EDGE + g * HALF, n * EDGE + (g + 1) * HALF)
                for m in range(HARM):
                    value = radial if m == 0 else radial * harmonics[m]
                    terms[pl.ds(start + m * TILE, 16), depth] = value.astype(BF16)
        return carry

    lax.fori_loop(0, TILE // 16, forward, 0)

    middle_row = HARM * TILE // 2
    env[:middle_row, :] = contract(terms[:middle_row, :], mix[...], ((1,), (0,)))
    env[middle_row:, :] = contract(terms[middle_row:, :], mix[...], ((1,), (0,)))

    def band(first, last):
        total = None
        for m in range(first, last):
            value = env[m * TILE : (m + 1) * TILE, :]
            total = value * value if total is None else total + value * value
        return total

    zeroth = band(0, 1)
    vector = band(1, 4)
    tensor = band(4, 9)
    for t in range(4):
        rows = slice(t * TILE, (t + 1) * TILE)
        cols = slice((t // 2) * 128, (t // 2) * 128 + 128)
        if t % 2 == 0:
            low = jnp.where(left_half, zeroth[:, cols], swap(vector[:, cols]))
            high = jnp.where(left_half, tensor[:, cols], centre_emb[rows])
        else:
            low = jnp.where(left_half, swap(zeroth[:, cols]), vector[:, cols])
            high = jnp.where(left_half, swap(tensor[:, cols]), centre_emb[rows])
        features[rows, 0:128] = low.astype(BF16)
        features[rows, 128:256] = high.astype(BF16)

    load_first.wait()
    before = contract(features[...], w_first[...], ((1,), (0,)))
    gate = 0.5 + 0.5 * jnp.tanh(0.5 * before)
    value = before * gate
    hidden[...] = value.astype(BF16)
    slope[...] = gate + value * (1.0 - gate)
    load_second.wait()
    before = contract(hidden[...], w_second[...], ((1,), (0,)))
    gate = 0.5 + 0.5 * jnp.tanh(0.5 * before)
    value = before * gate
    hidden[...] = value.astype(BF16)

    load_out.wait()
    w_out_parts = [part.astype(F32) for part in three_parts(out_ref[...])]
    turn = ((gate + value * (1.0 - gate)) * w_out_parts[0]).astype(BF16)
    turn = contract(turn, w_second[...], ((1,), (1,)))
    turn = (turn * slope[...]).astype(BF16)
    turn = contract(turn, w_first[...], ((1,), (1,)))
    for h in range(2):
        even = turn[2 * h * TILE : (2 * h + 1) * TILE]
        odd = turn[(2 * h + 1) * TILE : (2 * h + 2) * TILE]
        cols = slice(h * 128, (h + 1) * 128)
        pulls = [
            2.0 * jnp.where(left_half, even[:, 0:128], swap(odd[:, 0:128])),
            2.0 * jnp.where(left_half, swap(even[:, 0:128]), odd[:, 0:128]),
            2.0 * jnp.where(left_half, even[:, 128:256], swap(odd[:, 128:256])),
        ]
        for m in range(HARM):
            rows = slice(m * TILE, (m + 1) * TILE)
            kind = 0 if m == 0 else (1 if m < 4 else 2)
            env_grad[rows, cols] = (env[rows, cols] * pulls[kind]).astype(BF16)

    back_terms[...] = contract(env_grad[...], mix[...], ((1,), (1,)))

    push[...] = jnp.zeros(push.shape, F32)
    pull[3 * TILE :, :] = jnp.zeros((TILE, EDGE), F32)

    def backward(step, carry):
        start = pl.multiple_of(step * 8, 8)
        rows = pl.ds(start, 8)
        for g in range(2):
            cols = slice(g * HALF, (g + 1) * HALF)
            ux = edges[E_UX, rows, cols]
            uy = edges[E_UY, rows, cols]
            uz = edges[E_UZ, rows, cols]
            distance = edges[E_D, rows, cols]
            inverse = edges[E_INV, rows, cols]
            envelope = edges[E_F, rows, cols]
            harmonics = [
                None,
                ux,
                uy,
                uz,
                ux * uy,
                uy * uz,
                1.5 * uz * uz - 0.5,
                ux * uz,
                0.5 * (ux * ux - uy * uy),
            ]
            turned = [None] * HARM
            plain = None
            spotted = None
            for n in range(NB):
                bump = edges[n, rows, cols]
                depth = slice(n * EDGE + g * HALF, n * EDGE + (g + 1) * HALF)
                along = None
                for m in range(HARM):
                    value = back_terms[pl.ds(start + m * TILE, 8), depth]
                    if m == 0:
                        along = value
                    else:
                        along = along + value * harmonics[m]
                        piece = value * bump
                        turned[m] = piece if n == 0 else turned[m] + piece
                along = along * bump
                plain = along if n == 0 else plain + along
                spotted = along * spots[n] if n == 0 else spotted + along * spots[n]
            to_x = turned[1] + turned[4] * uy + turned[7] * uz + turned[8] * ux
            to_y = turned[2] + turned[4] * ux + turned[5] * uz - turned[8] * uy
            to_z = turned[3] + turned[5] * uy + 3.0 * turned[6] * uz + turned[7] * ux
            scaled = envelope * inverse
            by_d = -2.0 * sharpness * (distance * plain - spotted) * envelope
            by_d = by_d - (to_x * ux + to_y * uy + to_z * uz) * scaled
            by_q = -2.0 / cutoff_sq * plain * edges[E_SLOPE, rows, cols]
            radial = by_d + 2.0 * distance * by_q
            for axis, to, unit in ((0, to_x, ux), (1, to_y, uy), (2, to_z, uz)):
                flow = to * scaled + unit * radial
                pull[pl.ds(start + axis * TILE, 8), cols] = flow
                push[axis, :, cols] = push[axis, :, cols] + flow
        return carry

    lax.fori_loop(0, TILE // 8, backward, 0)

    folded = []
    for axis in range(3):
        total = jnp.sum(push[axis], axis=0, keepdims=True)
        spread_out = jnp.where(pair_mask, total, 0.0)
        narrow = (
            spread_out[:, 0:128]
            + spread_out[:, 128:256]
            + spread_out[:, 256:384]
            + spread_out[:, 384:512]
        )
        folded.append(narrow + swap(narrow))
    grads = jnp.concatenate(
        [
            jnp.where(left_half, folded[0], folded[1]),
            jnp.where(left_half, folded[2], 0.0),
            jnp.where(left_half, 0.0, folded[2]),
        ],
        axis=0,
    )
    message_row = iota((1, 256), 1)
    message_part = jnp.bitwise_and(message_row, 7)
    message_base = lax.shift_right_logical(message_row, 3) * 4
    flat = jnp.where(message_part < 4, message_base + message_part, -100)
    deep = jnp.where(
        (message_part == 4) | (message_part == 5), message_base + 2 * (message_part - 4), -100
    )
    want_wide = jnp.concatenate([want, want], axis=1)
    owner = jnp.concatenate(
        [(want_wide == rows.astype(F32)).astype(F32) for rows in (flat, deep, deep + 1)], axis=0
    ).astype(BF16)
    owed = None
    for piece in three_parts(grads):
        term = contract(owner, piece, ((0,), (0,)))
        owed = term if owed is None else owed + term
    for k in range(27):
        back_out[k] = owed[8 * k : 8 * k + 8]
    returns = []
    for a, b, c in around:
        landing = block_of(-a, -b, -c)
        copy = remote(
            back_out.at[block_of(a, b, c), pl.ds(0, 6)],
            back_in.at[landing, pl.ds(0, 6)],
            (a, b, c),
            19 + landing,
        )
        copy.start()
        returns.append((copy, landing))

    centre_grad = None
    for piece in three_parts(pull[...]):
        term = contract(centre_hot, piece, ((1,), (1,)))
        centre_grad = term if centre_grad is None else centre_grad + term

    w_out_rows = jnp.concatenate(w_out_parts + [jnp.zeros((13, hidden.shape[1]), F32)], axis=0)
    energy = contract(w_out_rows.astype(BF16), hidden[...], ((1,), (1,)))
    energy = energy[0:1] + energy[1:2] + energy[2:3]
    force_ref[3] = jnp.where(kinds >= 0, -energy, 0.0)

    own_block = block_of(0, 0, 0)
    gradient = owed[8 * own_block : 8 * own_block + 6]
    for copy, landing in returns:
        copy.wait_recv()
        gradient = gradient + back_in[landing, 0:6]

    centre_xy = centre_grad[0:4, 0:128]
    centre_z = centre_grad[0:4, 128:256]
    centre_z_swap = swap(centre_z)
    xy = gradient[0:4] - centre_xy
    xy_swap = swap(xy)
    for h in range(2):
        cols = slice(h * 128, (h + 1) * 128)
        even = slice(2 * h, 2 * h + 1)
        odd = slice(2 * h + 1, 2 * h + 2)
        force_ref[0, 0:1, cols] = jnp.where(left_half, xy[even], xy_swap[odd])
        force_ref[1, 0:1, cols] = jnp.where(left_half, xy_swap[even], xy[odd])
        force_ref[2, 0:1, cols] = gradient[4 + h : 5 + h] - jnp.where(
            left_half, centre_z[even], centre_z_swap[odd]
        )

    for copy in ask + fetch:
        copy.wait_send()
    for copy, *_ in ghosts + rims:
        copy.wait_send()
    for copy, _ in returns:
        copy.wait_send()


def local(sizes, positions, species, lists, sent, pairs, total, radial, emb, first, second, out):
    hidden = first.shape[1]
    vmem = pl.BlockSpec(memory_space=pltpu.VMEM)
    anywhere = pl.BlockSpec(memory_space=pltpu.HBM)
    both = pl.pallas_call(
        functools.partial(kernel, sizes),
        out_shape=jax.ShapeDtypeStruct((4, 1, 4 * TILE), F32),
        in_specs=[anywhere] * 11,
        out_specs=vmem,
        scratch_shapes=[
            pltpu.VMEM((3, 1, 128), F32),
            pltpu.VMEM((1, 128), jnp.int32),
            pltpu.VMEM((2, 64), jnp.int32),
            pltpu.SMEM((1, 2), jnp.int32),
            pltpu.SMEM((2, PAIRS), jnp.int32),
            pltpu.SMEM((1, 1, 1), jnp.int32),
            pltpu.VMEM(radial.shape, F32),
            pltpu.VMEM(emb.shape, F32),
            pltpu.VMEM((1, hidden), F32),
            pltpu.VMEM((8, 128), F32),
            pltpu.VMEM((15, 4, 256), F32),
            pltpu.VMEM((2, 1, 256), F32),
            pltpu.VMEM((6, 1, 256), F32),
            pltpu.VMEM((64, 256), F32),
            pltpu.VMEM((8, 128), F32),
            pltpu.VMEM((2, 8, 128), F32),
            pltpu.VMEM((2, 8, 256), F32),
            pltpu.VMEM((2, 8, 256), F32),
            pltpu.VMEM((27, 8, 128), F32),
            pltpu.VMEM((27, 8, 128), F32),
            pltpu.VMEM(first.shape, BF16),
            pltpu.VMEM(second.shape, BF16),
            pltpu.VMEM((NB * EDGE, 256), BF16),
            pltpu.VMEM((HARM * TILE, NB * EDGE), BF16),
            pltpu.VMEM((HARM * TILE, NB * EDGE), F32),
            pltpu.VMEM((NB + 7, TILE, EDGE), F32),
            pltpu.VMEM((4 * TILE, EDGE), F32),
            pltpu.VMEM((HARM * TILE, 256), F32),
            pltpu.VMEM((HARM * TILE, 256), BF16),
            pltpu.VMEM((256, 256), BF16),
            pltpu.VMEM((256, hidden), BF16),
            pltpu.VMEM((256, hidden), F32),
            pltpu.VMEM((4 * TILE, EDGE), F32),
            pltpu.VMEM((3, 8, EDGE), F32),
            pltpu.SemaphoreType.DMA((44,)),
            pltpu.SemaphoreType.DMA((46,)),
            pltpu.SemaphoreType.DMA((11,)),
        ],
        compiler_params=pltpu.CompilerParams(
            collective_id=0, has_side_effects=True, vmem_limit_bytes=56 * 1024 * 1024
        ),
    )(
        positions.reshape(3, 1, 128),
        species.reshape(1, 128),
        lists.reshape(2, 64),
        sent.reshape(1, 2),
        pairs.reshape(PAIRS, 2).T,
        total,
        radial,
        emb,
        out.reshape(1, hidden),
        first,
        second,
    )
    return -both[:3].reshape(1, 1, 1, 3, 4 * TILE), -both[3].reshape(1, 1, 1, 4 * TILE)


def solution(mesh):
    sizes = dict(mesh.shape)
    placed = (
        P("gx", "gy", "gz", None, None),
        P("gx", "gy", "gz", None),
        P("gx", "gy", "gz", None, None),
        P("gx", "gy", "gz", None),
        P("gx", "gy", "gz", None, None),
        P("gx", "gy", "gz"),
        P(),
        P(),
        P(),
        P(),
        P(),
    )
    return jax.shard_map(
        functools.partial(local, sizes),
        mesh=mesh,
        in_specs=placed,
        out_specs=(P("gx", "gy", "gz", None, None), P("gx", "gy", "gz", None)),
        check_vma=False,
    )
```

```python
import functools

import jax
import jax.numpy as jnp
from jax import lax
from jax.experimental import pallas as pl
from jax.experimental.pallas import tpu as pltpu
from jax.sharding import PartitionSpec as P

TILE = 64
NB = 8
PAIRS = 8
SPECIES = 8
CHANNELS = 64
HARM = 9
EDGE = PAIRS * TILE
HALF = EDGE // 2

cell = 10.0
cutoff = 5.0
cutoff_sq = 25.0
soften = 0.25
sharpness = 1.0
env_scale = 0.5

MESH = pl.DeviceIdType.MESH
F32 = jnp.float32
BF16 = jnp.bfloat16

PLANE_FAR = [(a, b) for a in (-2, -1, 0, 1, 2) for b in (-1, 0, 1)]

E_UX, E_UY, E_UZ, E_XY, E_YZ, E_ZZ, E_XZ, E_XX, E_D, E_INV, E_F, E_SLOPE = range(NB, NB + 12)


def slot_far(a, b):
    return (a + 2) * 3 + (b + 1)


def block_of(a, b, c):
    return (a + 1) * 9 + (b + 1) * 3 + (c + 1)


def iota(shape, dim):
    return lax.broadcasted_iota(jnp.int32, shape, dim)


def three_parts(value):
    high = value.astype(BF16)
    rest = value - high.astype(F32)
    middle = rest.astype(BF16)
    low = (rest - middle.astype(F32)).astype(BF16)
    return high, middle, low


def pick(hot, value, dims):
    total = None
    for part in three_parts(value):
        term = lax.dot_general(hot, part, (dims, ((), ())), preferred_element_type=F32)
        total = term if total is None else total + term
    return total


def contract(left, right, dims):
    return lax.dot_general(left, right, (dims, ((), ())), preferred_element_type=F32)


def kernel(
    sizes,
    pos_hbm,
    kind_hbm,
    list_hbm,
    sent_hbm,
    pair_hbm,
    total_hbm,
    radial_hbm,
    emb_hbm,
    out_hbm,
    first_hbm,
    second_hbm,
    force_ref,
    pos_ref,
    kind_ref,
    list_ref,
    sent_ref,
    pair_ref,
    total_ref,
    radial_ref,
    emb_ref,
    out_ref,
    packed,
    raw,
    rim_out,
    rim_in,
    plane,
    asked_own,
    asked,
    tiles_out,
    tiles_in,
    back_out,
    back_in,
    w_first,
    w_second,
    mix,
    terms,
    turned,
    edges,
    centre_at,
    env,
    env_grad,
    features,
    hidden,
    slope,
    pull,
    push,
    send_sem,
    recv_sem,
    load_sem,
):
    here = {axis: lax.axis_index(axis) for axis in ("gx", "gy", "gz")}

    def at(a, b, c):
        return {
            axis: lax.rem(here[axis] + (step + sizes[axis]), sizes[axis])
            for axis, step in (("gx", a), ("gy", b), ("gz", c))
        }

    far = [where for where in PLANE_FAR if where != (0, 0)]
    around = [(a, b, c) for c in (-1, 1, 0) for a in (-1, 0, 1) for b in (-1, 0, 1)]
    around.remove((0, 0, 0))

    barrier = pltpu.get_barrier_semaphore()
    for c in (-1, 1):
        pl.semaphore_signal(barrier, inc=1, device_id=at(0, 0, c), device_id_type=MESH)
    for a, b in far:
        pl.semaphore_signal(barrier, inc=1, device_id=at(a, b, 0), device_id_type=MESH)

    loads = []
    for src, dst in (
        (list_hbm, list_ref),
        (pos_hbm, pos_ref),
        (kind_hbm, kind_ref),
        (sent_hbm, sent_ref),
        (pair_hbm, pair_ref),
        (total_hbm, total_ref),
        (emb_hbm, emb_ref),
        (radial_hbm, radial_ref),
        (first_hbm, w_first),
        (second_hbm, w_second),
        (out_hbm, out_ref),
    ):
        copy = pltpu.make_async_copy(src, dst, load_sem.at[len(loads)])
        copy.start()
        loads.append(copy)
    load_emb, load_radial, load_first, load_second, load_out = loads[6:]
    plane[...] = jnp.zeros(plane.shape, F32)
    for copy in loads[:6]:
        copy.wait()

    counter = [0]

    def remote(src, dst, where, landing):
        index = counter[0]
        counter[0] += 1
        return pltpu.make_async_remote_copy(
            src_ref=src,
            dst_ref=dst,
            send_sem=send_sem.at[index],
            recv_sem=recv_sem.at[landing],
            device_id=at(*where),
            device_id_type=MESH,
        )

    lane = iota((1, 2 * TILE), 1)
    left_half = lane < TILE
    sub = iota((8, 2 * TILE), 0)

    def swap(value):
        return pltpu.roll(value, TILE, axis=value.ndim - 1)

    packed[0:1, :] = pos_ref[0]
    packed[1:2, :] = pos_ref[1]
    packed[2:3, :] = pos_ref[2]
    packed[3:4, :] = kind_ref[...].astype(F32)
    packed[4:8, :] = jnp.zeros((4, 2 * TILE), F32)
    atoms = packed[...]
    lists = list_ref[...]
    named = jnp.concatenate([lists[1:2], lists[0:1]], axis=1)
    live_lanes = jnp.where(left_half, sent_ref[0, 1], sent_ref[0, 0] + TILE)
    live = (lane < live_lanes).astype(F32)
    hot = (iota((2 * TILE, 2 * TILE), 0) == named).astype(F32).astype(BF16)
    leaving = contract(
        jnp.broadcast_to(live, (16, 2 * TILE)).astype(BF16), hot, ((1,), (1,))
    )[0:8]
    stacked = jnp.concatenate([part.astype(F32) for part in three_parts(atoms)], axis=0)
    stacked = jnp.concatenate([stacked, jnp.zeros((8, 2 * TILE), F32)], axis=0).astype(BF16)
    moved = contract(stacked, hot, ((1,), (0,)))
    moved = moved[0:8] + moved[8:16] + moved[16:24]
    moved = jnp.where((sub == 3) & (live < 0.5), -1.0, moved)
    staying = jnp.where((sub == 3) & (leaving > 0.5), -1.0, atoms)
    own = slot_far(0, 0)
    moved_swap = swap(moved)
    staying_swap = swap(staying)

    def put_row(row, one, other):
        raw[own, row : row + 1, 0:128] = jnp.where(left_half, one[0:1], other[1:2])
        raw[own, row : row + 1, 128:256] = jnp.where(left_half, one[2:3], other[3:4])

    put_row(0, moved, moved_swap)
    put_row(1, staying, staying_swap)
    put_row(2, staying_swap, staying)
    put_row(3, moved_swap, moved)
    rim_out[0] = raw[own, 0:1, :]
    rim_out[1] = raw[own, 3:4, :]

    pair_total = total_ref[0, 0, 0]
    want = jnp.full((8, 128), -1, jnp.int32)
    want_centre = jnp.full((8, 128), -1, jnp.int32)
    level = jnp.zeros((8, 128), jnp.int32)
    centres = []
    for p in range(PAIRS):
        active = p < pair_total
        centre = jnp.where(active, pair_ref[0, p], -1)
        other = jnp.where(active, pair_ref[1, p], -1)
        centres.append(centre)
        want = jnp.where(sub == p, other, want)
        want_centre = jnp.where(sub == p, jnp.where(active, centre + 13 * 4, -1), want_centre)
        level = jnp.where(sub == p, lax.rem(lax.div(other + 12, 4), 3) - 1, level)
    want = want.astype(F32)
    want_centre = want_centre.astype(F32)
    asked_own[...] = want

    pl.semaphore_wait(barrier, len(far) + 2)

    ask = [
        remote(asked_own, asked.at[1], (0, 0, -1), 0),
        remote(asked_own, asked.at[0], (0, 0, 1), 1),
    ]
    for copy in ask:
        copy.start()
    ghosts = []
    rims = []
    for a, b in sorted(far, key=lambda where: -abs(where[0])):
        landing = slot_far(-a, -b)
        if abs(a) == 2:
            side = 0 if a > 0 else 1
            place = side * 3 + (1 - b)
            copy = remote(rim_out.at[side], rim_in.at[place], (a, b, 0), 2 + landing)
            rims.append((copy, place, side, -a, -b))
        else:
            copy = remote(raw.at[own], raw.at[landing], (a, b, 0), 2 + landing)
            ghosts.append((copy, -a, -b))
        copy.start()

    load_emb.wait()
    load_radial.wait()
    wide = iota((1, 4 * TILE), 1)
    tile_of_lane = lax.shift_right_logical(wide, 6)
    emb = emb_ref[...]
    emb_twice = jnp.concatenate([emb, emb], axis=1)
    radial_twice = jnp.concatenate([radial_ref[...], radial_ref[...]], axis=1)
    emb_wide = jnp.concatenate([emb_twice, emb_twice], axis=1) * env_scale
    radial_wide = jnp.concatenate([radial_twice, radial_twice], axis=1)
    chosen = [(tile_of_lane == centres[p]).astype(F32) for p in range(PAIRS)]
    table = []
    for n in range(NB):
        base = emb_wide * radial_wide[n : n + 1]
        table.append(
            jnp.concatenate([base * chosen[p] for p in range(PAIRS)], axis=0).astype(BF16)
        )

    edge_lane = iota((8, EDGE), 1)
    edge_pair = lax.shift_right_logical(edge_lane, 6)
    pair_mask = edge_pair == iota((8, EDGE), 0)
    pair_hot = pair_mask.astype(F32)

    wide_xy = lax.shift_right_logical(wide, 6)

    def shifted(a, b):
        return jnp.where(wide_xy == 0, a * cell, 0.0) + jnp.where(wide_xy == 1, b * cell, 0.0)

    plane[4 * own : 4 * own + 4, :] = raw[own]
    for copy, a, b in ghosts:
        copy.wait_recv()
        k = slot_far(a, b)
        plane[4 * k : 4 * k + 4, :] = raw[k] + shifted(float(a), float(b))
    for copy, place, side, a, b in rims:
        copy.wait_recv()
        k = 4 * slot_far(a, b) + 3 * side
        plane[k : k + 1, :] = rim_in[place] + shifted(float(a), float(b))
    for copy in ask:
        copy.wait_recv()

    row = iota((1, 64), 1)
    part = jnp.bitwise_and(row, 3)
    block = lax.shift_right_logical(row, 2)
    far_x = lax.shift_right_logical(block * 11, 5)
    far_y = block - far_x * 3
    near_x = far_x - 1 + (part == 0).astype(jnp.int32) - (part == 3).astype(jnp.int32)
    raw_ok = (near_x >= 0) & (near_x <= 2) & (block < 15)
    raw_base = jnp.where(raw_ok, (9 * near_x + 3 * far_y) * 4 + part, -100)

    def asked_rows(base, parts):
        return jnp.concatenate(
            [
                (values[:, :64] == (base + 4 * (c + 1)).astype(F32)).astype(F32)
                for values, c in parts
            ],
            axis=0,
        ).astype(BF16)

    lower = asked[0]
    upper = asked[1]
    which = asked_rows(raw_base, [(want, 0), (lower, 1), (upper, -1), (want_centre, 0)])
    picked = pick(which, plane[...], ((1,), (0,)))
    tiles_out[0] = picked[8:16]
    tiles_out[1] = picked[16:24]
    fetch = [
        remote(tiles_out.at[0], tiles_in.at[1], (0, 0, -1), 17),
        remote(tiles_out.at[1], tiles_in.at[0], (0, 0, 1), 18),
    ]
    for copy in fetch:
        copy.start()

    pair_hot16 = pair_hot.astype(BF16)
    spread = None
    for piece in three_parts(picked[24:32]):
        term = contract(piece, pair_hot16, ((0,), (0,)))
        spread = term if spread is None else spread + term
    centre_at[...] = spread

    tile_rows = [
        plane[4 * slot_far(-1, 0) : 4 * slot_far(-1, 0) + 1, 128:256],
        plane[4 * own + 1 : 4 * own + 2, 128:256],
        plane[4 * own + 2 : 4 * own + 3, 128:256],
        plane[4 * slot_far(1, 0) + 3 : 4 * slot_far(1, 0) + 4, 128:256],
    ]
    kinds = jnp.concatenate(
        [
            jnp.where(left_half, swap(tile_rows[0]), tile_rows[1]),
            jnp.where(left_half, swap(tile_rows[2]), tile_rows[3]),
        ],
        axis=1,
    )
    kind_hot = (kinds == iota((SPECIES, 256), 0).astype(F32)).astype(F32).astype(BF16)
    centre_emb = contract(kind_hot, emb_twice.astype(BF16), ((0,), (0,)))

    def pair_row(values):
        tiled = jnp.concatenate([values] * 4, axis=1)
        return jnp.sum(jnp.where(pair_mask, tiled, 0.0), axis=0, keepdims=True)

    same = pair_row((want == want_centre).astype(F32))
    centre_row = jnp.zeros((1, EDGE), jnp.int32) - 1
    for p in range(PAIRS):
        centre_row = jnp.where(edge_pair[0:1] == p, centres[p], centre_row)
    centre_hot = (centre_row == iota((16, EDGE), 0)).astype(F32).astype(BF16)
    lane_j = jnp.bitwise_and(edge_lane[0:1], TILE - 1)

    for copy in fetch:
        copy.wait_recv()
    lift = jnp.where(left_half, level.astype(F32) * cell, 0.0)
    others = picked[0:8] + tiles_in[0] + tiles_in[1]
    xy = others[:, :128]
    zs = others[:, 128:256] + lift
    xy_swap = swap(xy)
    zs_swap = swap(zs)
    other_x = pair_row(jnp.where(left_half, xy, xy_swap))
    other_y = pair_row(jnp.where(left_half, xy_swap, xy))
    other_z = pair_row(jnp.where(left_half, zs, zs_swap))
    other_kind = pair_row(jnp.where(left_half, zs_swap, zs))
    other_live = (other_kind >= 0).astype(F32)

    kind_rows = iota((SPECIES, EDGE), 0).astype(F32)
    of_kind = (other_kind == kind_rows).astype(F32)
    other_hot = jnp.concatenate(
        [of_kind * (edge_pair == p).astype(F32) for p in range(PAIRS)], axis=0
    ).astype(BF16)
    for n in range(NB):
        mix[n * EDGE : (n + 1) * EDGE, :] = contract(
            other_hot, table[n], ((0,), (0,))
        ).astype(BF16)

    spots = [cutoff * (n + 1) / NB for n in range(NB)]

    def forward(step, carry):
        start = pl.multiple_of(step * 16, 16)
        rows = pl.ds(start, 16)
        row_i = iota((16, HALF), 0) + start
        for g in range(2):
            cols = slice(g * HALF, (g + 1) * HALF)
            dx = other_x[:, cols] - centre_at[pl.ds(start, 16), cols]
            dy = other_y[:, cols] - centre_at[pl.ds(start + TILE, 16), cols]
            dz = other_z[:, cols] - centre_at[pl.ds(start + 2 * TILE, 16), cols]
            kind_i = centre_at[pl.ds(start + 3 * TILE, 16), cols]
            squared = dx * dx + dy * dy + dz * dz
            inverse = lax.rsqrt(squared + soften)
            distance = (squared + soften) * inverse
            keep = jnp.where(kind_i >= 0, other_live[:, cols], 0.0)
            keep = jnp.where((row_i == lane_j[:, cols]) & (same[:, cols] > 0.5), 0.0, keep)
            inside = jnp.maximum(1.0 - squared * (1.0 / cutoff_sq), 0.0)
            slope_f = inside * keep
            envelope = inside * slope_f
            ux = dx * inverse
            uy = dy * inverse
            uz = dz * inverse
            edges[E_UX, rows, cols] = ux
            edges[E_UY, rows, cols] = uy
            edges[E_UZ, rows, cols] = uz
            edges[E_D, rows, cols] = distance
            edges[E_INV, rows, cols] = inverse
            edges[E_F, rows, cols] = envelope
            edges[E_SLOPE, rows, cols] = slope_f
            edges[E_XY, rows, cols] = ux * uy
            edges[E_YZ, rows, cols] = uy * uz
            edges[E_ZZ, rows, cols] = 1.5 * uz * uz - 0.5
            edges[E_XZ, rows, cols] = ux * uz
            edges[E_XX, rows, cols] = 0.5 * (ux * ux - uy * uy)
        return carry

    lax.fori_loop(0, TILE // 16, forward, 0)

    middle_row = HARM * TILE // 2
    sums = [None, None]
    for n in range(NB):
        away = edges[E_D] - spots[n]
        bump = jnp.exp(-sharpness * away * away)
        edges[n] = bump
        radial = bump * edges[E_F]
        cols = slice(n * EDGE, (n + 1) * EDGE)
        for m in range(HARM):
            value = radial if m == 0 else radial * edges[E_UX + m - 1]
            terms[m * TILE : (m + 1) * TILE, cols] = value.astype(BF16)
        for h in range(2):
            part_rows = slice(h * middle_row, (h + 1) * middle_row)
            term = contract(terms[part_rows, cols], mix[cols, :], ((1,), (0,)))
            sums[h] = term if n == 0 else sums[h] + term
    env[:middle_row, :] = sums[0]
    env[middle_row:, :] = sums[1]

    def band(first, last):
        total = None
        for m in range(first, last):
            value = env[m * TILE : (m + 1) * TILE, :]
            total = value * value if total is None else total + value * value
        return total

    zeroth = band(0, 1)
    vector = band(1, 4)
    tensor = band(4, 9)
    for t in range(4):
        rows = slice(t * TILE, (t + 1) * TILE)
        cols = slice((t // 2) * 128, (t // 2) * 128 + 128)
        if t % 2 == 0:
            low = jnp.where(left_half, zeroth[:, cols], swap(vector[:, cols]))
            high = jnp.where(left_half, tensor[:, cols], centre_emb[rows])
        else:
            low = jnp.where(left_half, swap(zeroth[:, cols]), vector[:, cols])
            high = jnp.where(left_half, swap(tensor[:, cols]), centre_emb[rows])
        features[rows, 0:128] = low.astype(BF16)
        features[rows, 128:256] = high.astype(BF16)

    load_first.wait()
    before = contract(features[...], w_first[...], ((1,), (0,)))
    gate = 0.5 + 0.5 * jnp.tanh(0.5 * before)
    value = before * gate
    hidden[...] = value.astype(BF16)
    slope[...] = gate + value * (1.0 - gate)
    load_second.wait()
    before = contract(hidden[...], w_second[...], ((1,), (0,)))
    gate = 0.5 + 0.5 * jnp.tanh(0.5 * before)
    value = before * gate
    hidden[...] = value.astype(BF16)

    load_out.wait()
    w_out_parts = [part.astype(F32) for part in three_parts(out_ref[...])]
    turn = ((gate + value * (1.0 - gate)) * w_out_parts[0]).astype(BF16)
    turn = contract(turn, w_second[...], ((1,), (1,)))
    turn = (turn * slope[...]).astype(BF16)
    turn = contract(turn, w_first[...], ((1,), (1,)))
    for h in range(2):
        even = turn[2 * h * TILE : (2 * h + 1) * TILE]
        odd = turn[(2 * h + 1) * TILE : (2 * h + 2) * TILE]
        cols = slice(h * 128, (h + 1) * 128)
        pulls = [
            2.0 * jnp.where(left_half, even[:, 0:128], swap(odd[:, 0:128])),
            2.0 * jnp.where(left_half, swap(even[:, 0:128]), odd[:, 0:128]),
            2.0 * jnp.where(left_half, even[:, 128:256], swap(odd[:, 128:256])),
        ]
        for m in range(HARM):
            rows = slice(m * TILE, (m + 1) * TILE)
            kind = 0 if m == 0 else (1 if m < 4 else 2)
            env_grad[rows, cols] = (env[rows, cols] * pulls[kind]).astype(BF16)

    for n in range(NB):
        bump = edges[n]
        cols = slice(n * EDGE, (n + 1) * EDGE)
        back = contract(env_grad[...], mix[cols, :], ((1,), (1,)))
        along = None
        for m in range(HARM):
            value = back[m * TILE : (m + 1) * TILE]
            piece = value * bump
            turned[m] = piece if n == 0 else turned[m] + piece
            along = piece if m == 0 else along + piece * edges[E_UX + m - 1]
        along = along * spots[n]
        turned[HARM] = along if n == 0 else turned[HARM] + along

    push[...] = jnp.zeros(push.shape, F32)
    pull[3 * TILE :, :] = jnp.zeros((TILE, EDGE), F32)

    def backward(step, carry):
        start = pl.multiple_of(step * 8, 8)
        rows = pl.ds(start, 8)
        for g in range(2):
            cols = slice(g * HALF, (g + 1) * HALF)
            ux = edges[E_UX, rows, cols]
            uy = edges[E_UY, rows, cols]
            uz = edges[E_UZ, rows, cols]
            distance = edges[E_D, rows, cols]
            envelope = edges[E_F, rows, cols]
            to = [turned[m, rows, cols] for m in range(HARM)]
            plain = to[0]
            for m in range(1, HARM):
                plain = plain + to[m] * edges[E_UX + m - 1, rows, cols]
            to_x = to[1] + to[4] * uy + to[7] * uz + to[8] * ux
            to_y = to[2] + to[4] * ux + to[5] * uz - to[8] * uy
            to_z = to[3] + to[5] * uy + 3.0 * to[6] * uz + to[7] * ux
            scaled = envelope * edges[E_INV, rows, cols]
            by_d = -2.0 * sharpness * (distance * plain - turned[HARM, rows, cols]) * envelope
            by_d = by_d - (to_x * ux + to_y * uy + to_z * uz) * scaled
            by_q = -2.0 / cutoff_sq * plain * edges[E_SLOPE, rows, cols]
            radial = by_d + 2.0 * distance * by_q
            for axis, side, unit in ((0, to_x, ux), (1, to_y, uy), (2, to_z, uz)):
                flow = side * scaled + unit * radial
                pull[pl.ds(start + axis * TILE, 8), cols] = flow
                push[axis, :, cols] = push[axis, :, cols] + flow
        return carry

    lax.fori_loop(0, TILE // 8, backward, 0)

    folded = []
    for axis in range(3):
        total = jnp.sum(push[axis], axis=0, keepdims=True)
        spread_out = jnp.where(pair_mask, total, 0.0)
        narrow = (
            spread_out[:, 0:128]
            + spread_out[:, 128:256]
            + spread_out[:, 256:384]
            + spread_out[:, 384:512]
        )
        folded.append(narrow + swap(narrow))
    grads = jnp.concatenate(
        [
            jnp.where(left_half, folded[0], folded[1]),
            jnp.where(left_half, folded[2], 0.0),
            jnp.where(left_half, 0.0, folded[2]),
        ],
        axis=0,
    )
    message_row = iota((1, 256), 1)
    message_part = jnp.bitwise_and(message_row, 7)
    message_base = lax.shift_right_logical(message_row, 3) * 4
    flat = jnp.where(message_part < 4, message_base + message_part, -100)
    deep = jnp.where(
        (message_part == 4) | (message_part == 5), message_base + 2 * (message_part - 4), -100
    )
    want_wide = jnp.concatenate([want, want], axis=1)
    owner = jnp.concatenate(
        [(want_wide == rows.astype(F32)).astype(F32) for rows in (flat, deep, deep + 1)], axis=0
    ).astype(BF16)
    owed = None
    for piece in three_parts(grads):
        term = contract(owner, piece, ((0,), (0,)))
        owed = term if owed is None else owed + term
    for k in range(27):
        back_out[k] = owed[8 * k : 8 * k + 8]
    returns = []
    for a, b, c in around:
        landing = block_of(-a, -b, -c)
        copy = remote(
            back_out.at[block_of(a, b, c), pl.ds(0, 6)],
            back_in.at[landing, pl.ds(0, 6)],
            (a, b, c),
            19 + landing,
        )
        copy.start()
        returns.append((copy, landing))

    centre_grad = None
    for piece in three_parts(pull[...]):
        term = contract(centre_hot, piece, ((1,), (1,)))
        centre_grad = term if centre_grad is None else centre_grad + term

    w_out_rows = jnp.concatenate(w_out_parts + [jnp.zeros((13, hidden.shape[1]), F32)], axis=0)
    energy = contract(w_out_rows.astype(BF16), hidden[...], ((1,), (1,)))
    energy = energy[0:1] + energy[1:2] + energy[2:3]
    force_ref[3] = jnp.where(kinds >= 0, -energy, 0.0)

    own_block = block_of(0, 0, 0)
    gradient = owed[8 * own_block : 8 * own_block + 6]
    for copy, landing in returns:
        copy.wait_recv()
        gradient = gradient + back_in[landing, 0:6]

    centre_xy = centre_grad[0:4, 0:128]
    centre_z = centre_grad[0:4, 128:256]
    centre_z_swap = swap(centre_z)
    xy = gradient[0:4] - centre_xy
    xy_swap = swap(xy)
    for h in range(2):
        cols = slice(h * 128, (h + 1) * 128)
        even = slice(2 * h, 2 * h + 1)
        odd = slice(2 * h + 1, 2 * h + 2)
        force_ref[0, 0:1, cols] = jnp.where(left_half, xy[even], xy_swap[odd])
        force_ref[1, 0:1, cols] = jnp.where(left_half, xy_swap[even], xy[odd])
        force_ref[2, 0:1, cols] = gradient[4 + h : 5 + h] - jnp.where(
            left_half, centre_z[even], centre_z_swap[odd]
        )

    for copy in ask + fetch:
        copy.wait_send()
    for copy, *_ in ghosts + rims:
        copy.wait_send()
    for copy, _ in returns:
        copy.wait_send()


def local(sizes, positions, species, lists, sent, pairs, total, radial, emb, first, second, out):
    hidden = first.shape[1]
    vmem = pl.BlockSpec(memory_space=pltpu.VMEM)
    anywhere = pl.BlockSpec(memory_space=pltpu.HBM)
    both = pl.pallas_call(
        functools.partial(kernel, sizes),
        out_shape=jax.ShapeDtypeStruct((4, 1, 4 * TILE), F32),
        in_specs=[anywhere] * 11,
        out_specs=vmem,
        scratch_shapes=[
            pltpu.VMEM((3, 1, 128), F32),
            pltpu.VMEM((1, 128), jnp.int32),
            pltpu.VMEM((2, 64), jnp.int32),
            pltpu.SMEM((1, 2), jnp.int32),
            pltpu.SMEM((2, PAIRS), jnp.int32),
            pltpu.SMEM((1, 1, 1), jnp.int32),
            pltpu.VMEM(radial.shape, F32),
            pltpu.VMEM(emb.shape, F32),
            pltpu.VMEM((1, hidden), F32),
            pltpu.VMEM((8, 128), F32),
            pltpu.VMEM((15, 4, 256), F32),
            pltpu.VMEM((2, 1, 256), F32),
            pltpu.VMEM((6, 1, 256), F32),
            pltpu.VMEM((64, 256), F32),
            pltpu.VMEM((8, 128), F32),
            pltpu.VMEM((2, 8, 128), F32),
            pltpu.VMEM((2, 8, 256), F32),
            pltpu.VMEM((2, 8, 256), F32),
            pltpu.VMEM((27, 8, 128), F32),
            pltpu.VMEM((27, 8, 128), F32),
            pltpu.VMEM(first.shape, BF16),
            pltpu.VMEM(second.shape, BF16),
            pltpu.VMEM((NB * EDGE, 256), BF16),
            pltpu.VMEM((HARM * TILE, NB * EDGE), BF16),
            pltpu.VMEM((HARM + 1, TILE, EDGE), F32),
            pltpu.VMEM((NB + 12, TILE, EDGE), F32),
            pltpu.VMEM((4 * TILE, EDGE), F32),
            pltpu.VMEM((HARM * TILE, 256), F32),
            pltpu.VMEM((HARM * TILE, 256), BF16),
            pltpu.VMEM((256, 256), BF16),
            pltpu.VMEM((256, hidden), BF16),
            pltpu.VMEM((256, hidden), F32),
            pltpu.VMEM((4 * TILE, EDGE), F32),
            pltpu.VMEM((3, 8, EDGE), F32),
            pltpu.SemaphoreType.DMA((44,)),
            pltpu.SemaphoreType.DMA((46,)),
            pltpu.SemaphoreType.DMA((11,)),
        ],
        compiler_params=pltpu.CompilerParams(
            collective_id=0, has_side_effects=True, vmem_limit_bytes=56 * 1024 * 1024
        ),
    )(
        positions.reshape(3, 1, 128),
        species.reshape(1, 128),
        lists.reshape(2, 64),
        sent.reshape(1, 2),
        pairs.reshape(PAIRS, 2).T,
        total,
        radial,
        emb,
        out.reshape(1, hidden),
        first,
        second,
    )
    return -both[:3].reshape(1, 1, 1, 3, 4 * TILE), -both[3].reshape(1, 1, 1, 4 * TILE)


def solution(mesh):
    sizes = dict(mesh.shape)
    placed = (
        P("gx", "gy", "gz", None, None),
        P("gx", "gy", "gz", None),
        P("gx", "gy", "gz", None, None),
        P("gx", "gy", "gz", None),
        P("gx", "gy", "gz", None, None),
        P("gx", "gy", "gz"),
        P(),
        P(),
        P(),
        P(),
        P(),
    )
    return jax.shard_map(
        functools.partial(local, sizes),
        mesh=mesh,
        in_specs=placed,
        out_specs=(P("gx", "gy", "gz", None, None), P("gx", "gy", "gz", None)),
        check_vma=False,
    )
```

```python
import functools

import jax
import jax.numpy as jnp
from jax import lax
from jax.experimental import pallas as pl
from jax.experimental.pallas import tpu as pltpu
from jax.sharding import PartitionSpec as P

TILE = 64
NB = 8
PAIRS = 8
SPECIES = 8
CHANNELS = 64
HARM = 9
EDGE = PAIRS * TILE
HALF = EDGE // 2

cell = 10.0
cutoff = 5.0
cutoff_sq = 25.0
soften = 0.25
sharpness = 1.0
env_scale = 0.5

MESH = pl.DeviceIdType.MESH
F32 = jnp.float32
BF16 = jnp.bfloat16

PLANE_FAR = [(a, b) for a in (-2, -1, 0, 1, 2) for b in (-1, 0, 1)]

E_UX, E_UY, E_UZ, E_XY, E_YZ, E_ZZ, E_XZ, E_XX, E_D, E_INV, E_F, E_SLOPE = range(NB, NB + 12)


def slot_far(a, b):
    return (a + 2) * 3 + (b + 1)


def block_of(a, b, c):
    return (a + 1) * 9 + (b + 1) * 3 + (c + 1)


def iota(shape, dim):
    return lax.broadcasted_iota(jnp.int32, shape, dim)


def three_parts(value):
    high = value.astype(BF16)
    rest = value - high.astype(F32)
    middle = rest.astype(BF16)
    low = (rest - middle.astype(F32)).astype(BF16)
    return high, middle, low


def pick(hot, value, dims):
    total = None
    for part in three_parts(value):
        term = lax.dot_general(hot, part, (dims, ((), ())), preferred_element_type=F32)
        total = term if total is None else total + term
    return total


def contract(left, right, dims):
    return lax.dot_general(left, right, (dims, ((), ())), preferred_element_type=F32)


def kernel(
    sizes,
    pos_hbm,
    kind_hbm,
    list_hbm,
    sent_hbm,
    pair_hbm,
    total_hbm,
    radial_hbm,
    emb_hbm,
    out_hbm,
    first_hbm,
    second_hbm,
    force_ref,
    pos_ref,
    kind_ref,
    list_ref,
    sent_ref,
    pair_ref,
    total_ref,
    radial_ref,
    emb_ref,
    out_ref,
    packed,
    raw,
    rim_out,
    rim_in,
    plane,
    asked_own,
    asked,
    tiles_out,
    tiles_in,
    back_out,
    back_in,
    w_first,
    w_second,
    mix,
    terms,
    turned,
    edges,
    centre_at,
    env,
    env_grad,
    features,
    hidden,
    pull,
    push,
    send_sem,
    recv_sem,
    load_sem,
):
    here = {axis: lax.axis_index(axis) for axis in ("gx", "gy", "gz")}

    def at(a, b, c):
        return {
            axis: lax.rem(here[axis] + (step + sizes[axis]), sizes[axis])
            for axis, step in (("gx", a), ("gy", b), ("gz", c))
        }

    far = [where for where in PLANE_FAR if where != (0, 0)]
    around = [(a, b, c) for a in (-1, 1, 0) for b in (-1, 0, 1) for c in (-1, 1)]
    around += [(a, b, 0) for a in (-1, 1, 0) for b in (-1, 0, 1)]
    around.remove((0, 0, 0))

    barrier = pltpu.get_barrier_semaphore()
    for c in (-1, 1):
        pl.semaphore_signal(barrier, inc=1, device_id=at(0, 0, c), device_id_type=MESH)
    for a, b in far:
        pl.semaphore_signal(barrier, inc=1, device_id=at(a, b, 0), device_id_type=MESH)

    loads = []
    for src, dst in (
        (list_hbm, list_ref),
        (pos_hbm, pos_ref),
        (kind_hbm, kind_ref),
        (sent_hbm, sent_ref),
        (pair_hbm, pair_ref),
        (total_hbm, total_ref),
        (emb_hbm, emb_ref),
        (radial_hbm, radial_ref),
        (first_hbm, w_first),
        (second_hbm, w_second),
        (out_hbm, out_ref),
    ):
        copy = pltpu.make_async_copy(src, dst, load_sem.at[len(loads)])
        copy.start()
        loads.append(copy)
    load_emb, load_radial, load_first, load_second, load_out = loads[6:]
    plane[...] = jnp.zeros(plane.shape, F32)
    for copy in loads[:6]:
        copy.wait()

    counter = [0]

    def remote(src, dst, where, landing):
        index = counter[0]
        counter[0] += 1
        return pltpu.make_async_remote_copy(
            src_ref=src,
            dst_ref=dst,
            send_sem=send_sem.at[index],
            recv_sem=recv_sem.at[landing],
            device_id=at(*where),
            device_id_type=MESH,
        )

    lane = iota((1, 2 * TILE), 1)
    left_half = lane < TILE
    sub = iota((8, 2 * TILE), 0)

    def swap(value):
        return pltpu.roll(value, TILE, axis=value.ndim - 1)

    packed[0:1, :] = pos_ref[0]
    packed[1:2, :] = pos_ref[1]
    packed[2:3, :] = pos_ref[2]
    packed[3:4, :] = kind_ref[...].astype(F32)
    packed[4:8, :] = jnp.zeros((4, 2 * TILE), F32)
    atoms = packed[...]
    lists = list_ref[...]
    named = jnp.concatenate([lists[1:2], lists[0:1]], axis=1)
    live_lanes = jnp.where(left_half, sent_ref[0, 1], sent_ref[0, 0] + TILE)
    live = (lane < live_lanes).astype(F32)
    hot = (iota((2 * TILE, 2 * TILE), 0) == named).astype(F32).astype(BF16)
    leaving = contract(
        jnp.broadcast_to(live, (16, 2 * TILE)).astype(BF16), hot, ((1,), (1,))
    )[0:8]
    stacked = jnp.concatenate([part.astype(F32) for part in three_parts(atoms)], axis=0)
    stacked = jnp.concatenate([stacked, jnp.zeros((8, 2 * TILE), F32)], axis=0).astype(BF16)
    moved = contract(stacked, hot, ((1,), (0,)))
    moved = moved[0:8] + moved[8:16] + moved[16:24]
    moved = jnp.where((sub == 3) & (live < 0.5), -1.0, moved)
    staying = jnp.where((sub == 3) & (leaving > 0.5), -1.0, atoms)
    own = slot_far(0, 0)
    moved_swap = swap(moved)
    staying_swap = swap(staying)

    def put_row(row, one, other):
        raw[own, row : row + 1, 0:128] = jnp.where(left_half, one[0:1], other[1:2])
        raw[own, row : row + 1, 128:256] = jnp.where(left_half, one[2:3], other[3:4])

    put_row(0, moved, moved_swap)
    put_row(1, staying, staying_swap)
    put_row(2, staying_swap, staying)
    put_row(3, moved_swap, moved)
    rim_out[0] = raw[own, 0:1, :]
    rim_out[1] = raw[own, 3:4, :]

    pair_total = total_ref[0, 0, 0]
    want = jnp.full((8, 128), -1, jnp.int32)
    want_centre = jnp.full((8, 128), -1, jnp.int32)
    level = jnp.zeros((8, 128), jnp.int32)
    centres = []
    for p in range(PAIRS):
        active = p < pair_total
        centre = jnp.where(active, pair_ref[0, p], -1)
        other = jnp.where(active, pair_ref[1, p], -1)
        centres.append(centre)
        want = jnp.where(sub == p, other, want)
        want_centre = jnp.where(sub == p, jnp.where(active, centre + 13 * 4, -1), want_centre)
        level = jnp.where(sub == p, lax.rem(lax.div(other + 12, 4), 3) - 1, level)
    want = want.astype(F32)
    want_centre = want_centre.astype(F32)
    asked_own[...] = want

    pl.semaphore_wait(barrier, len(far) + 2)

    ask = [
        remote(asked_own, asked.at[1], (0, 0, -1), 0),
        remote(asked_own, asked.at[0], (0, 0, 1), 1),
    ]
    for copy in ask:
        copy.start()
    ghosts = []
    rims = []
    for a, b in sorted(far, key=lambda where: -abs(where[0])):
        landing = slot_far(-a, -b)
        if abs(a) == 2:
            side = 0 if a > 0 else 1
            place = side * 3 + (1 - b)
            copy = remote(rim_out.at[side], rim_in.at[place], (a, b, 0), 2 + landing)
            rims.append((copy, place, side, -a, -b))
        else:
            copy = remote(raw.at[own], raw.at[landing], (a, b, 0), 2 + landing)
            ghosts.append((copy, -a, -b))
        copy.start()

    load_emb.wait()
    load_radial.wait()
    wide = iota((1, 4 * TILE), 1)
    tile_of_lane = lax.shift_right_logical(wide, 6)
    emb = emb_ref[...]
    emb_twice = jnp.concatenate([emb, emb], axis=1)
    radial_twice = jnp.concatenate([radial_ref[...], radial_ref[...]], axis=1)
    emb_wide = jnp.concatenate([emb_twice, emb_twice], axis=1) * env_scale
    radial_wide = jnp.concatenate([radial_twice, radial_twice], axis=1)
    chosen = [(tile_of_lane == centres[p]).astype(F32) for p in range(PAIRS)]
    table = []
    for n in range(NB):
        base = emb_wide * radial_wide[n : n + 1]
        table.append(
            jnp.concatenate([base * chosen[p] for p in range(PAIRS)], axis=0).astype(BF16)
        )

    edge_lane = iota((8, EDGE), 1)
    edge_pair = lax.shift_right_logical(edge_lane, 6)
    pair_mask = edge_pair == iota((8, EDGE), 0)
    pair_hot = pair_mask.astype(F32)

    wide_xy = lax.shift_right_logical(wide, 6)

    def shifted(a, b):
        return jnp.where(wide_xy == 0, a * cell, 0.0) + jnp.where(wide_xy == 1, b * cell, 0.0)

    plane[4 * own : 4 * own + 4, :] = raw[own]
    for copy, a, b in ghosts:
        copy.wait_recv()
        k = slot_far(a, b)
        plane[4 * k : 4 * k + 4, :] = raw[k] + shifted(float(a), float(b))
    for copy, place, side, a, b in rims:
        copy.wait_recv()
        k = 4 * slot_far(a, b) + 3 * side
        plane[k : k + 1, :] = rim_in[place] + shifted(float(a), float(b))
    for copy in ask:
        copy.wait_recv()

    row = iota((1, 64), 1)
    part = jnp.bitwise_and(row, 3)
    block = lax.shift_right_logical(row, 2)
    far_x = lax.shift_right_logical(block * 11, 5)
    far_y = block - far_x * 3
    near_x = far_x - 1 + (part == 0).astype(jnp.int32) - (part == 3).astype(jnp.int32)
    raw_ok = (near_x >= 0) & (near_x <= 2) & (block < 15)
    raw_base = jnp.where(raw_ok, (9 * near_x + 3 * far_y) * 4 + part, -100)

    def asked_rows(base, parts):
        return jnp.concatenate(
            [
                (values[:, :64] == (base + 4 * (c + 1)).astype(F32)).astype(F32)
                for values, c in parts
            ],
            axis=0,
        ).astype(BF16)

    lower = asked[0]
    upper = asked[1]
    which = asked_rows(raw_base, [(want, 0), (lower, 1), (upper, -1), (want_centre, 0)])
    picked = pick(which, plane[...], ((1,), (0,)))
    tiles_out[0] = picked[8:16]
    tiles_out[1] = picked[16:24]
    fetch = [
        remote(tiles_out.at[0], tiles_in.at[1], (0, 0, -1), 17),
        remote(tiles_out.at[1], tiles_in.at[0], (0, 0, 1), 18),
    ]
    for copy in fetch:
        copy.start()

    pair_hot16 = pair_hot.astype(BF16)
    spread = None
    for piece in three_parts(picked[24:32]):
        term = contract(piece, pair_hot16, ((0,), (0,)))
        spread = term if spread is None else spread + term
    centre_at[...] = spread

    tile_rows = [
        plane[4 * slot_far(-1, 0) : 4 * slot_far(-1, 0) + 1, 128:256],
        plane[4 * own + 1 : 4 * own + 2, 128:256],
        plane[4 * own + 2 : 4 * own + 3, 128:256],
        plane[4 * slot_far(1, 0) + 3 : 4 * slot_far(1, 0) + 4, 128:256],
    ]
    kinds = jnp.concatenate(
        [
            jnp.where(left_half, swap(tile_rows[0]), tile_rows[1]),
            jnp.where(left_half, swap(tile_rows[2]), tile_rows[3]),
        ],
        axis=1,
    )
    kind_hot = (kinds == iota((SPECIES, 256), 0).astype(F32)).astype(F32).astype(BF16)
    centre_emb = contract(kind_hot, emb_twice.astype(BF16), ((0,), (0,)))

    def pair_row(values):
        tiled = jnp.concatenate([values] * 4, axis=1)
        return jnp.sum(jnp.where(pair_mask, tiled, 0.0), axis=0, keepdims=True)

    same = pair_row((want == want_centre).astype(F32))
    centre_row = jnp.zeros((1, EDGE), jnp.int32) - 1
    for p in range(PAIRS):
        centre_row = jnp.where(edge_pair[0:1] == p, centres[p], centre_row)
    centre_hot = (centre_row == iota((16, EDGE), 0)).astype(F32).astype(BF16)
    lane_j = jnp.bitwise_and(edge_lane[0:1], TILE - 1)

    for copy in fetch:
        copy.wait_recv()
    lift = jnp.where(left_half, level.astype(F32) * cell, 0.0)
    others = picked[0:8] + tiles_in[0] + tiles_in[1]
    xy = others[:, :128]
    zs = others[:, 128:256] + lift
    xy_swap = swap(xy)
    zs_swap = swap(zs)
    other_x = pair_row(jnp.where(left_half, xy, xy_swap))
    other_y = pair_row(jnp.where(left_half, xy_swap, xy))
    other_z = pair_row(jnp.where(left_half, zs, zs_swap))
    other_kind = pair_row(jnp.where(left_half, zs_swap, zs))
    other_live = (other_kind >= 0).astype(F32)

    kind_rows = iota((SPECIES, EDGE), 0).astype(F32)
    of_kind = (other_kind == kind_rows).astype(F32)
    other_hot = jnp.concatenate(
        [of_kind * (edge_pair == p).astype(F32) for p in range(PAIRS)], axis=0
    ).astype(BF16)
    for n in range(NB):
        mix[n * EDGE : (n + 1) * EDGE, :] = contract(
            other_hot, table[n], ((0,), (0,))
        ).astype(BF16)

    spots = [cutoff * (n + 1) / NB for n in range(NB)]

    def forward(step, carry):
        start = pl.multiple_of(step * 16, 16)
        rows = pl.ds(start, 16)
        row_i = iota((16, HALF), 0) + start
        for g in range(2):
            cols = slice(g * HALF, (g + 1) * HALF)
            dx = other_x[:, cols] - centre_at[pl.ds(start, 16), cols]
            dy = other_y[:, cols] - centre_at[pl.ds(start + TILE, 16), cols]
            dz = other_z[:, cols] - centre_at[pl.ds(start + 2 * TILE, 16), cols]
            kind_i = centre_at[pl.ds(start + 3 * TILE, 16), cols]
            squared = dx * dx + dy * dy + dz * dz
            inverse = lax.rsqrt(squared + soften)
            distance = (squared + soften) * inverse
            keep = jnp.where(kind_i >= 0, other_live[:, cols], 0.0)
            keep = jnp.where((row_i == lane_j[:, cols]) & (same[:, cols] > 0.5), 0.0, keep)
            inside = jnp.maximum(1.0 - squared * (1.0 / cutoff_sq), 0.0)
            slope_f = inside * keep
            envelope = inside * slope_f
            ux = dx * inverse
            uy = dy * inverse
            uz = dz * inverse
            edges[E_UX, rows, cols] = ux
            edges[E_UY, rows, cols] = uy
            edges[E_UZ, rows, cols] = uz
            edges[E_D, rows, cols] = distance
            edges[E_INV, rows, cols] = inverse
            edges[E_F, rows, cols] = envelope
            edges[E_SLOPE, rows, cols] = slope_f
            edges[E_XY, rows, cols] = ux * uy
            edges[E_YZ, rows, cols] = uy * uz
            edges[E_ZZ, rows, cols] = 1.5 * uz * uz - 0.5
            edges[E_XZ, rows, cols] = ux * uz
            edges[E_XX, rows, cols] = 0.5 * (ux * ux - uy * uy)
        return carry

    lax.fori_loop(0, TILE // 16, forward, 0)

    middle_row = HARM * TILE // 2
    sums = [None, None]
    for n in range(NB):
        away = edges[E_D] - spots[n]
        bump = jnp.exp(-sharpness * away * away)
        edges[n] = bump
        radial = bump * edges[E_F]
        cols = slice(n * EDGE, (n + 1) * EDGE)
        for m in range(HARM):
            value = radial if m == 0 else radial * edges[E_UX + m - 1]
            terms[m * TILE : (m + 1) * TILE, cols] = value.astype(BF16)
        for h in range(2):
            part_rows = slice(h * middle_row, (h + 1) * middle_row)
            term = contract(terms[part_rows, cols], mix[cols, :], ((1,), (0,)))
            sums[h] = term if n == 0 else sums[h] + term
    env[:middle_row, :] = sums[0]
    env[middle_row:, :] = sums[1]

    def band(first, last):
        total = None
        for m in range(first, last):
            value = env[m * TILE : (m + 1) * TILE, :]
            total = value * value if total is None else total + value * value
        return total

    zeroth = band(0, 1)
    vector = band(1, 4)
    tensor = band(4, 9)
    for t in range(4):
        rows = slice(t * TILE, (t + 1) * TILE)
        cols = slice((t // 2) * 128, (t // 2) * 128 + 128)
        if t % 2 == 0:
            low = jnp.where(left_half, zeroth[:, cols], swap(vector[:, cols]))
            high = jnp.where(left_half, tensor[:, cols], centre_emb[rows])
        else:
            low = jnp.where(left_half, swap(zeroth[:, cols]), vector[:, cols])
            high = jnp.where(left_half, swap(tensor[:, cols]), centre_emb[rows])
        features[rows, 0:128] = low.astype(BF16)
        features[rows, 128:256] = high.astype(BF16)

    load_first.wait()
    load_second.wait()
    load_out.wait()
    w_out_parts = [part.astype(F32) for part in three_parts(out_ref[...])]
    turns = []
    for h in range(2):
        rows = slice(2 * h * TILE, 2 * (h + 1) * TILE)
        before = contract(features[rows, :], w_first[...], ((1,), (0,)))
        gate = 0.5 + 0.5 * jnp.tanh(0.5 * before)
        value = before * gate
        bend = gate + value * (1.0 - gate)
        before = contract(value.astype(BF16), w_second[...], ((1,), (0,)))
        gate = 0.5 + 0.5 * jnp.tanh(0.5 * before)
        value = before * gate
        hidden[rows, :] = value.astype(BF16)

        turn = ((gate + value * (1.0 - gate)) * w_out_parts[0]).astype(BF16)
        turn = contract(turn, w_second[...], ((1,), (1,)))
        turn = (turn * bend).astype(BF16)
        turns.append(contract(turn, w_first[...], ((1,), (1,))))
    for h in range(2):
        even = turns[h][:TILE]
        odd = turns[h][TILE:]
        cols = slice(h * 128, (h + 1) * 128)
        pulls = [
            2.0 * jnp.where(left_half, even[:, 0:128], swap(odd[:, 0:128])),
            2.0 * jnp.where(left_half, swap(even[:, 0:128]), odd[:, 0:128]),
            2.0 * jnp.where(left_half, even[:, 128:256], swap(odd[:, 128:256])),
        ]
        for m in range(HARM):
            rows = slice(m * TILE, (m + 1) * TILE)
            kind = 0 if m == 0 else (1 if m < 4 else 2)
            env_grad[rows, cols] = (env[rows, cols] * pulls[kind]).astype(BF16)

    for n in range(NB):
        bump = edges[n]
        cols = slice(n * EDGE, (n + 1) * EDGE)
        back = contract(env_grad[...], mix[cols, :], ((1,), (1,)))
        along = None
        for m in range(HARM):
            value = back[m * TILE : (m + 1) * TILE]
            piece = value * bump
            turned[m] = piece if n == 0 else turned[m] + piece
            along = piece if m == 0 else along + piece * edges[E_UX + m - 1]
        along = along * spots[n]
        turned[HARM] = along if n == 0 else turned[HARM] + along

    push[...] = jnp.zeros(push.shape, F32)
    pull[3 * TILE :, :] = jnp.zeros((TILE, EDGE), F32)

    def backward(step, carry):
        start = pl.multiple_of(step * 8, 8)
        rows = pl.ds(start, 8)
        for g in range(2):
            cols = slice(g * HALF, (g + 1) * HALF)
            ux = edges[E_UX, rows, cols]
            uy = edges[E_UY, rows, cols]
            uz = edges[E_UZ, rows, cols]
            distance = edges[E_D, rows, cols]
            envelope = edges[E_F, rows, cols]
            to = [turned[m, rows, cols] for m in range(HARM)]
            plain = to[0]
            for m in range(1, HARM):
                plain = plain + to[m] * edges[E_UX + m - 1, rows, cols]
            to_x = to[1] + to[4] * uy + to[7] * uz + to[8] * ux
            to_y = to[2] + to[4] * ux + to[5] * uz - to[8] * uy
            to_z = to[3] + to[5] * uy + 3.0 * to[6] * uz + to[7] * ux
            scaled = envelope * edges[E_INV, rows, cols]
            by_d = -2.0 * sharpness * (distance * plain - turned[HARM, rows, cols]) * envelope
            by_d = by_d - (to_x * ux + to_y * uy + to_z * uz) * scaled
            by_q = -2.0 / cutoff_sq * plain * edges[E_SLOPE, rows, cols]
            radial = by_d + 2.0 * distance * by_q
            for axis, side, unit in ((0, to_x, ux), (1, to_y, uy), (2, to_z, uz)):
                flow = side * scaled + unit * radial
                pull[pl.ds(start + axis * TILE, 8), cols] = flow
                push[axis, :, cols] = push[axis, :, cols] + flow
        return carry

    lax.fori_loop(0, TILE // 8, backward, 0, unroll=4)

    folded = []
    for axis in range(3):
        total = jnp.sum(push[axis], axis=0, keepdims=True)
        spread_out = jnp.where(pair_mask, total, 0.0)
        narrow = (
            spread_out[:, 0:128]
            + spread_out[:, 128:256]
            + spread_out[:, 256:384]
            + spread_out[:, 384:512]
        )
        folded.append(narrow + swap(narrow))
    grads = jnp.concatenate(
        [
            jnp.where(left_half, folded[0], folded[1]),
            jnp.where(left_half, folded[2], 0.0),
            jnp.where(left_half, 0.0, folded[2]),
        ],
        axis=0,
    )
    message_row = iota((1, 256), 1)
    message_part = jnp.bitwise_and(message_row, 7)
    message_base = lax.shift_right_logical(message_row, 3) * 4
    flat = jnp.where(message_part < 4, message_base + message_part, -100)
    deep = jnp.where(
        (message_part == 4) | (message_part == 5), message_base + 2 * (message_part - 4), -100
    )
    want_wide = jnp.concatenate([want, want], axis=1)
    owner = jnp.concatenate(
        [(want_wide == rows.astype(F32)).astype(F32) for rows in (flat, deep, deep + 1)], axis=0
    ).astype(BF16)
    owed = None
    for piece in three_parts(grads):
        term = contract(owner, piece, ((0,), (0,)))
        owed = term if owed is None else owed + term
    for k in range(27):
        back_out[k] = owed[8 * k : 8 * k + 8]
    returns = []
    for a, b, c in around:
        landing = block_of(-a, -b, -c)
        copy = remote(
            back_out.at[block_of(a, b, c), pl.ds(0, 6)],
            back_in.at[landing, pl.ds(0, 6)],
            (a, b, c),
            19 + landing,
        )
        copy.start()
        returns.append((copy, landing))

    centre_grad = None
    for piece in three_parts(pull[...]):
        term = contract(centre_hot, piece, ((1,), (1,)))
        centre_grad = term if centre_grad is None else centre_grad + term

    w_out_rows = jnp.concatenate(w_out_parts + [jnp.zeros((13, hidden.shape[1]), F32)], axis=0)
    energy = contract(w_out_rows.astype(BF16), hidden[...], ((1,), (1,)))
    energy = energy[0:1] + energy[1:2] + energy[2:3]
    force_ref[3] = jnp.where(kinds >= 0, -energy, 0.0)

    own_block = block_of(0, 0, 0)
    gradient = owed[8 * own_block : 8 * own_block + 6]
    for copy, landing in returns:
        copy.wait_recv()
        gradient = gradient + back_in[landing, 0:6]

    centre_xy = centre_grad[0:4, 0:128]
    centre_z = centre_grad[0:4, 128:256]
    centre_z_swap = swap(centre_z)
    xy = gradient[0:4] - centre_xy
    xy_swap = swap(xy)
    for h in range(2):
        cols = slice(h * 128, (h + 1) * 128)
        even = slice(2 * h, 2 * h + 1)
        odd = slice(2 * h + 1, 2 * h + 2)
        force_ref[0, 0:1, cols] = jnp.where(left_half, xy[even], xy_swap[odd])
        force_ref[1, 0:1, cols] = jnp.where(left_half, xy_swap[even], xy[odd])
        force_ref[2, 0:1, cols] = gradient[4 + h : 5 + h] - jnp.where(
            left_half, centre_z[even], centre_z_swap[odd]
        )

    for copy in ask + fetch:
        copy.wait_send()
    for copy, *_ in ghosts + rims:
        copy.wait_send()
    for copy, _ in returns:
        copy.wait_send()


def local(sizes, positions, species, lists, sent, pairs, total, radial, emb, first, second, out):
    hidden = first.shape[1]
    vmem = pl.BlockSpec(memory_space=pltpu.VMEM)
    anywhere = pl.BlockSpec(memory_space=pltpu.HBM)
    both = pl.pallas_call(
        functools.partial(kernel, sizes),
        out_shape=pltpu.VMEM((4, 1, 4 * TILE), F32),
        in_specs=[anywhere] * 11,
        out_specs=vmem,
        scratch_shapes=[
            pltpu.VMEM((3, 1, 128), F32),
            pltpu.VMEM((1, 128), jnp.int32),
            pltpu.VMEM((2, 64), jnp.int32),
            pltpu.SMEM((1, 2), jnp.int32),
            pltpu.SMEM((2, PAIRS), jnp.int32),
            pltpu.SMEM((1, 1, 1), jnp.int32),
            pltpu.VMEM(radial.shape, F32),
            pltpu.VMEM(emb.shape, F32),
            pltpu.VMEM((1, hidden), F32),
            pltpu.VMEM((8, 128), F32),
            pltpu.VMEM((15, 4, 256), F32),
            pltpu.VMEM((2, 1, 256), F32),
            pltpu.VMEM((6, 1, 256), F32),
            pltpu.VMEM((64, 256), F32),
            pltpu.VMEM((8, 128), F32),
            pltpu.VMEM((2, 8, 128), F32),
            pltpu.VMEM((2, 8, 256), F32),
            pltpu.VMEM((2, 8, 256), F32),
            pltpu.VMEM((27, 8, 128), F32),
            pltpu.VMEM((27, 8, 128), F32),
            pltpu.VMEM(first.shape, BF16),
            pltpu.VMEM(second.shape, BF16),
            pltpu.VMEM((NB * EDGE, 256), BF16),
            pltpu.VMEM((HARM * TILE, NB * EDGE), BF16),
            pltpu.VMEM((HARM + 1, TILE, EDGE), F32),
            pltpu.VMEM((NB + 12, TILE, EDGE), F32),
            pltpu.VMEM((4 * TILE, EDGE), F32),
            pltpu.VMEM((HARM * TILE, 256), F32),
            pltpu.VMEM((HARM * TILE, 256), BF16),
            pltpu.VMEM((256, 256), BF16),
            pltpu.VMEM((256, hidden), BF16),
            pltpu.VMEM((4 * TILE, EDGE), F32),
            pltpu.VMEM((3, 8, EDGE), F32),
            pltpu.SemaphoreType.DMA((44,)),
            pltpu.SemaphoreType.DMA((46,)),
            pltpu.SemaphoreType.DMA((11,)),
        ],
        compiler_params=pltpu.CompilerParams(
            collective_id=0, has_side_effects=True, vmem_limit_bytes=56 * 1024 * 1024
        ),
    )(
        positions.reshape(3, 1, 128),
        species.reshape(1, 128),
        lists.reshape(2, 64),
        sent.reshape(1, 2),
        pairs.reshape(PAIRS, 2).T,
        total,
        radial,
        emb,
        out.reshape(1, hidden),
        first,
        second,
    )
    return -both[:3].reshape(1, 1, 1, 3, 4 * TILE), -both[3].reshape(1, 1, 1, 4 * TILE)


def solution(mesh):
    sizes = dict(mesh.shape)
    placed = (
        P("gx", "gy", "gz", None, None),
        P("gx", "gy", "gz", None),
        P("gx", "gy", "gz", None, None),
        P("gx", "gy", "gz", None),
        P("gx", "gy", "gz", None, None),
        P("gx", "gy", "gz"),
        P(),
        P(),
        P(),
        P(),
        P(),
    )
    return jax.shard_map(
        functools.partial(local, sizes),
        mesh=mesh,
        in_specs=placed,
        out_specs=(P("gx", "gy", "gz", None, None), P("gx", "gy", "gz", None)),
        check_vma=False,
    )
```
